32 devices in a mesh: dp: 8 (over y, x, core), tensor: 4 (over z).
Axes of the slice: x: 2, y: 2, z: 4, core: 2. Of those that a mesh axis runs over, the one named last changes fastest.
Arguments:
- hidden_in: bfloat16 [8192, 1600], P(('dp', 'tensor')), may hold values from -6 to 6
- out_grad: bfloat16 [8192, 1600], P(('dp', 'tensor')), may hold values from -6 to 6
- segments: int32 [8192], P('dp'), may hold values from 0 to 2, as said below
- norm_input: bfloat16 [1600], P('dp'), may hold values from 0.25 to 1.75
- query_weight: bfloat16 [1600, 1600], P('dp'), may hold values from -0.15625 to 0.15625
- key_weight: bfloat16 [1600, 320], P('dp'), may hold values from -0.15625 to 0.15625
- value_weight: bfloat16 [1600, 320], P('dp'), may hold values from -0.15625 to 0.15625
- attn_out_weight: bfloat16 [1600, 1600], P('dp'), may hold values from -0.15625 to 0.15625
- norm_attn: bfloat16 [1600], P('dp'), may hold values from 0.25 to 1.75
- ssm_x_weight: bfloat16 [1600, 3200], P('dp', 'tensor'), may hold values from -0.15625 to 0.15625
- ssm_gate_weight: bfloat16 [1600, 3200], P('dp', 'tensor'), may hold values from -0.15625 to 0.15625
- ssm_bcd_weight: bfloat16 [1600, 132], P('dp'), may hold values from -0.15625 to 0.15625
- step_weight: bfloat16 [100, 3200], P(None, 'dp'), may hold values from -0.625 to 0.625
- step_bias: bfloat16 [3200], P('dp'), may hold values from -6.5 to -2.5
- decay_log: bfloat16 [3200], P('dp'), may hold values from -1 to 1.5
- skip_gain: bfloat16 [3200], P('dp'), may hold values from 0.5 to 1.5
- conv_weight: bfloat16 [4, 3200], P(None, 'dp'), may hold values from -3 to 3
- ssm_out_weight: bfloat16 [3200, 1600], P('tensor', 'dp'), may hold values from -0.109375 to 0.109375
- norm_ssm: bfloat16 [1600], P('dp'), may hold values from 0.25 to 1.75
- norm_ffn: bfloat16 [1600], P('dp'), may hold values from 0.25 to 1.75
- gate_weight: bfloat16 [1600, 5504], P('dp', 'tensor'), may hold values from -0.15625 to 0.15625
- up_weight: bfloat16 [1600, 5504], P('dp', 'tensor'), may hold values from -0.15625 to 0.15625
- down_weight: bfloat16 [5504, 1600], P('tensor', 'dp'), may hold values from -0.078125 to 0.078125
Outputs:
- layer_out: bfloat16 [8192, 1600], P(('dp', 'tensor'))
- grad_hidden_in: float32 [8192, 1600], P(('dp', 'tensor'))
- grad_norm_input: float32 [1600], P('dp')
- grad_query_weight: float32 [1600, 1600], P('dp')
- grad_key_weight: float32 [1600, 320], P('dp')
- grad_value_weight: float32 [1600, 320], P('dp')
- grad_attn_out_weight: float32 [1600, 1600], P('dp')
- grad_norm_attn: float32 [1600], P('dp')
- grad_ssm_x_weight: float32 [1600, 3200], P('dp', 'tensor')
- grad_ssm_gate_weight: float32 [1600, 3200], P('dp', 'tensor')
- grad_ssm_bcd_weight: float32 [1600, 132], P('dp')
- grad_step_weight: float32 [100, 3200], P(None, 'dp')
- grad_step_bias: float32 [3200], P('dp')
- grad_decay_log: float32 [3200], P('dp')
- grad_skip_gain: float32 [3200], P('dp')
- grad_conv_weight: float32 [4, 3200], P(None, 'dp')
- grad_ssm_out_weight: float32 [3200, 1600], P('tensor', 'dp')
- grad_norm_ssm: float32 [1600], P('dp')
- grad_norm_ffn: float32 [1600], P('dp')
- grad_gate_weight: float32 [1600, 5504], P('dp', 'tensor')
- grad_up_weight: float32 [1600, 5504], P('dp', 'tensor')
- grad_down_weight: float32 [5504, 1600], P('tensor', 'dp')
The draws below stay inside these ranges and needn't reach their ends.
Inputs may be any that keep to these rules, and one draw needn't show every extreme that they name: `segments`: in each aligned run of 1024 tokens the segment numbers are 0, then 1, then 2, never falling, each segment non-empty; segment 1 begins within the run's first 256 tokens and ends within its last 256.
All inputs are finite; a program needn't handle non-finite values.
Results may differ from the reference program's by a relative error of at most 0.024.
Values may be sent and summed in bfloat16 or wider, within the bound.
No kernel may reach another device: no remote copies, remote signals or barrier semaphores. Data moves between devices by JAX's collectives and lax.ppermute only.
A program may use at most 320 MiB of HBM per device.

```python
import jax
import jax.numpy as jnp
from jax import lax

D = 1600
KV_HEADS = 5
HEAD_DIM = 64
INNER = 3200
STATE = 16
STEP_RANK = 100
CONV = 4
FF = 5504
WINDOW = 1024
BLOCK = 16
GROUP = 1024
TOK_DEV = 256
TOKENS = 8192


def draw_segments(key, part):
    key = jax.random.fold_in(key, 7)
    first_key, last_key = jax.random.split(key)
    group_count = TOKENS // GROUP
    first_cut = jax.random.randint(first_key, (group_count, 1), 1, TOK_DEV)
    last_cut = jax.random.randint(last_key, (group_count, 1), GROUP - TOK_DEV + 1, GROUP)
    positions = jnp.arange(GROUP, dtype=jnp.int32)[None, :]
    labels = (positions >= first_cut).astype(jnp.int32) + (positions >= last_cut).astype(jnp.int32)
    return labels.reshape(TOKENS)


def shard_levels(stream_key, shape, shards, low, top_value):
    gain, own = 1.0, jax.random.fold_in(stream_key, 6)
    for position, blocks in shards:
        draws = jnp.exp(jax.random.uniform(jax.random.fold_in(own, position), (blocks,), jnp.float32, low / len(shards), top_value / len(shards)))
        gain = gain * jnp.repeat(draws, shape[position] // blocks).reshape([-1 if axis == position else 1 for axis in range(len(shape))])
    return gain


def noise(stream_key, extent, scale, bound, cuts=(), kind=jnp.bfloat16):
    values = scale * jax.random.normal(stream_key, extent, jnp.float32)
    if cuts:
        values = values * shard_levels(stream_key, extent, cuts, -0.22, 0.18)
    return jnp.clip(values, -bound, bound).astype(kind)


def setup_inputs(seed: int = 0) -> dict:
    streams_of = jax.random.split(jax.random.key(seed), 24)
    return {
        "hidden_in": noise(streams_of[0], (TOKENS, D), 1.0, 6.0, ((0, 32),)),
        "out_grad": noise(streams_of[1], (TOKENS, D), 1.0, 6.0, ((0, 32),)),
        "segments": draw_segments(jax.random.fold_in(streams_of[23], 71), 0),
        "norm_input": jnp.clip(1.0 + 0.15 * jax.random.normal(streams_of[3], (D,), jnp.float32), 0.25, 1.75).astype(jnp.bfloat16),
        "query_weight": noise(streams_of[4], (D, D), D ** -0.5, 0.15625, ((0, 8),)),
        "key_weight": noise(streams_of[5], (D, KV_HEADS * HEAD_DIM), D ** -0.5, 0.15625, ((0, 8),)),
        "value_weight": noise(streams_of[6], (D, KV_HEADS * HEAD_DIM), D ** -0.5, 0.15625, ((0, 8),)),
        "attn_out_weight": noise(streams_of[7], (D, D), D ** -0.5, 0.15625, ((0, 8),)),
        "norm_attn": jnp.clip(1.0 + 0.15 * jax.random.normal(streams_of[8], (D,), jnp.float32), 0.25, 1.75).astype(jnp.bfloat16),
        "ssm_x_weight": noise(streams_of[9], (D, INNER), D ** -0.5, 0.15625, ((0, 8), (1, 4))),
        "ssm_gate_weight": noise(streams_of[10], (D, INNER), D ** -0.5, 0.15625, ((0, 8), (1, 4))),
        "ssm_bcd_weight": noise(streams_of[11], (D, 2 * STATE + STEP_RANK), D ** -0.5, 0.15625, ((0, 8),)),
        "step_weight": noise(streams_of[12], (STEP_RANK, INNER), STEP_RANK ** -0.5, 0.625, ((1, 8),)),
        "step_bias": jnp.clip(-6.5 + 4.0 * jax.random.uniform(streams_of[13], (INNER,), jnp.float32) ** shard_levels(streams_of[13], (INNER,), ((0, 8),), -0.2, 0.2), -6.5, -2.5).astype(jnp.bfloat16),
        "decay_log": jnp.clip(-1.0 + 2.5 * jax.random.uniform(streams_of[14], (INNER,), jnp.float32) ** shard_levels(streams_of[14], (INNER,), ((0, 8),), -0.2, 0.2), -1.0, 1.5).astype(jnp.bfloat16),
        "skip_gain": jnp.clip(0.5 + 1.0 * jax.random.uniform(streams_of[15], (INNER,), jnp.float32) ** shard_levels(streams_of[15], (INNER,), ((0, 8),), -0.2, 0.2), 0.5, 1.5).astype(jnp.bfloat16),
        "conv_weight": noise(streams_of[16], (CONV, INNER), CONV ** -0.5, 3.0, ((1, 8),)),
        "ssm_out_weight": noise(streams_of[17], (INNER, D), INNER ** -0.5, 0.109375, ((0, 4), (1, 8))),
        "norm_ssm": jnp.clip(1.0 + 0.15 * jax.random.normal(streams_of[18], (D,), jnp.float32), 0.25, 1.75).astype(jnp.bfloat16),
        "norm_ffn": jnp.clip(1.0 + 0.15 * jax.random.normal(streams_of[19], (D,), jnp.float32), 0.25, 1.75).astype(jnp.bfloat16),
        "gate_weight": noise(streams_of[20], (D, FF), D ** -0.5, 0.15625, ((0, 8), (1, 4))),
        "up_weight": noise(streams_of[21], (D, FF), D ** -0.5, 0.15625, ((0, 8), (1, 4))),
        "down_weight": noise(streams_of[22], (FF, D), FF ** -0.5, 0.078125, ((0, 4), (1, 8))),
    }


epsilon = 1e-05
highest = lax.Precision.HIGHEST

@jax.custom_vjp
def low(v):
    return lax.optimization_barrier(v.astype(jnp.bfloat16)).astype(jnp.float32)

@jax.custom_vjp
def low_back(v):
    return v

def low_keep(v):
    return (low(v), None)

def low_pass(kept, grad):
    return (grad,)

def back_keep(v):
    return (v, None)

def back_low(kept, grad):
    return (low(grad),)
low.defvjp(low_keep, low_pass)
low_back.defvjp(back_keep, back_low)

def matmul(left_side, right_side):
    return jnp.dot(left_side, right_side, precision=highest, preferred_element_type=jnp.float32)

def rms_norm(values, gain_vec):
    return values * lax.rsqrt(lax.optimization_barrier(jnp.mean(values * values, axis=-1, keepdims=True)) + epsilon) * gain_vec

def ssm_scan(decay_rates, drives, b_input, c_output, seg_ids):
    length, channel_count = decay_rates.shape
    block_count = length // BLOCK
    rate_blocks = decay_rates.reshape(block_count, BLOCK, channel_count)
    drive_blocks = drives.reshape(block_count, BLOCK, channel_count)
    b_blocks = b_input.reshape(block_count, BLOCK, -1)
    c_blocks = c_output.reshape(block_count, BLOCK, -1)
    seg_blocks = seg_ids.reshape(block_count, BLOCK)
    log_decay = -jnp.cumsum(rate_blocks, axis=1)
    seg_last = seg_blocks[:, -1]
    seg_before = jnp.concatenate([jnp.full((1,), -1, jnp.int32), seg_last[:-1]])
    same_last = (seg_blocks == seg_last[:, None]).astype(jnp.float32)
    tail_weight = jnp.exp(log_decay[:, -1:, :] - log_decay) * same_last[:, :, None] * drive_blocks
    block_state = jnp.einsum('bsc,bsn->bcn', tail_weight, b_blocks, precision=highest)
    carry_gain = jnp.exp(log_decay[:, -1, :]) * (seg_last == seg_before).astype(jnp.float32)[:, None]

    def combine(earlier_pair, later_pair):
        return (earlier_pair[0] * later_pair[0], later_pair[0][..., None] * earlier_pair[1] + later_pair[1])
    _, states = lax.associative_scan(combine, (carry_gain, block_state))
    entering = jnp.concatenate([jnp.zeros_like(states[:1]), states[:-1]], 0)

    def one_block(pieces):
        log_block, drive_block, b_block, c_block, seg_block, seg_prior, state_in = pieces
        positions = jnp.arange(BLOCK)
        allowed = (positions[:, None] >= positions[None, :]) & (seg_block[:, None] == seg_block[None, :])
        intersection = jnp.dot(c_block, b_block.T, precision=highest, preferred_element_type=jnp.float32) * allowed.astype(jnp.float32)
        decay_table = jnp.exp(jnp.where(allowed[:, :, None], log_block[:, None, :] - log_block[None, :, :], -1e+30))
        inside_part = jnp.einsum('ts,tsc,sc->tc', intersection, decay_table, drive_block, precision=highest)
        carried = jnp.exp(log_block) * (seg_block == seg_prior).astype(jnp.float32)[:, None] * jnp.dot(c_block, state_in.T, precision=highest, preferred_element_type=jnp.float32)
        return inside_part + carried

    def grouped(values_in):
        return values_in.reshape((block_count // 4, 4) + values_in.shape[1:])
    outputs = lax.map(jax.checkpoint(jax.vmap(one_block)), tuple((grouped(item) for item in (log_decay, drive_blocks, b_blocks, c_blocks, seg_blocks, seg_before, entering))))
    return outputs.reshape(length, channel_count)

def ssm_branch(inner_in, gate_in, bcd_values, step_w, step_b, decay_l, skip_g, conv_w, seg_ids):
    length = inner_in.shape[0]
    conv_total = jnp.zeros_like(inner_in)
    for delay_index in range(conv_w.shape[0]):
        lagged = jnp.pad(inner_in, ((delay_index, 0), (0, 0)))[:length]
        lagged_seg = jnp.pad(seg_ids, (delay_index, 0), constant_values=-1)[:length]
        conv_total = conv_total + conv_w[delay_index] * jnp.where((lagged_seg == seg_ids)[:, None], lagged, 0.0)
    driven = jax.nn.silu(conv_total)
    b_input = bcd_values[:, :STATE]
    c_output = bcd_values[:, STATE:2 * STATE]
    step_low = bcd_values[:, 2 * STATE:]
    step_sizes = jax.nn.softplus(jnp.dot(step_low, step_w, precision=highest, preferred_element_type=jnp.float32) + step_b)
    decay_rates = step_sizes * jnp.exp(decay_l)
    scanned = ssm_scan(decay_rates, step_sizes * driven, b_input, c_output, seg_ids)
    return (scanned + skip_g * driven) * jax.nn.silu(gate_in)

def attention(queries, key_rows, value_rows, seg_ids):
    length = queries.shape[0]
    kv_groups = key_rows.shape[1] // HEAD_DIM
    repeat = queries.shape[1] // key_rows.shape[1]
    block_rows = min(512, length)
    query4 = queries.reshape(length, kv_groups, repeat, HEAD_DIM)
    key3 = key_rows.reshape(length, kv_groups, HEAD_DIM)
    value3 = value_rows.reshape(length, kv_groups, HEAD_DIM)
    key_pos = jnp.arange(length, dtype=jnp.int32)

    def one_block(row_start):
        rows = lax.dynamic_slice_in_dim(query4, row_start, block_rows, 0)
        scores = low_back(jnp.einsum('qgrd,kgd->grqk', rows, key3, precision=highest) * HEAD_DIM ** (-0.5))
        query_pos = row_start + jnp.arange(block_rows, dtype=jnp.int32)
        query_seg = lax.dynamic_slice_in_dim(seg_ids, row_start, block_rows, 0)
        allowed = (key_pos[None, :] <= query_pos[:, None]) & (query_pos[:, None] - key_pos[None, :] < WINDOW) & (query_seg[:, None] == seg_ids[None, :])
        scores = jnp.where(allowed[None, None], scores, -jnp.inf)
        probabilities = jax.nn.softmax(scores, axis=-1)
        mixed = jnp.einsum('grqk,kgd->qgrd', low(probabilities), value3, precision=highest)
        return low(low_back(mixed.reshape(block_rows, -1)))
    starts = jnp.arange(length // block_rows, dtype=jnp.int32) * block_rows
    return lax.map(jax.checkpoint(one_block), starts).reshape(length, -1)

def layer(params, values, seg_ids):
    norm_input, query_weight, key_weight, value_weight, attn_out_weight, norm_attn, ssm_x_weight, ssm_gate_weight, ssm_bcd_weight, step_weight, step_bias, decay_log, skip_gain, conv_weight, ssm_out_weight, norm_ssm, norm_ffn, gate_weight, up_weight, down_weight = params
    normed = low(rms_norm(values, norm_input))
    queries = low(low_back(matmul(normed, query_weight)))
    key_rows = low(low_back(matmul(normed, key_weight)))
    value_rows = low(low_back(matmul(normed, value_weight)))
    attended = attention(queries, key_rows, value_rows, seg_ids)
    attn_proj = low_back(matmul(attended, attn_out_weight))
    inner_in = low_back(matmul(normed, ssm_x_weight))
    gate_in = low_back(matmul(normed, ssm_gate_weight))
    bcd_values = matmul(normed, ssm_bcd_weight)
    gated_out = low(ssm_branch(inner_in, gate_in, bcd_values, step_weight, step_bias, decay_log, skip_gain, conv_weight, seg_ids))
    ssm_proj = low_back(matmul(gated_out, ssm_out_weight))
    residual = values + 0.5 * (rms_norm(attn_proj, norm_attn) + rms_norm(ssm_proj, norm_ssm))
    ffn_in = low(rms_norm(residual, norm_ffn))
    gate_pre = low_back(matmul(ffn_in, gate_weight))
    up_pre = low_back(matmul(ffn_in, up_weight))
    activated = low(jax.nn.silu(gate_pre) * up_pre)
    return residual + matmul(activated, down_weight)

def reference(hidden_in, out_grad, segments, norm_input, query_weight, key_weight, value_weight, attn_out_weight, norm_attn, ssm_x_weight, ssm_gate_weight, ssm_bcd_weight, step_weight, step_bias, decay_log, skip_gain, conv_weight, ssm_out_weight, norm_ssm, norm_ffn, gate_weight, up_weight, down_weight):
    weights = tuple((item.astype(jnp.float32) for item in (norm_input, query_weight, key_weight, value_weight, attn_out_weight, norm_attn, ssm_x_weight, ssm_gate_weight, ssm_bcd_weight, step_weight, step_bias, decay_log, skip_gain, conv_weight, ssm_out_weight, norm_ssm, norm_ffn, gate_weight, up_weight, down_weight)))
    group_count = TOKENS // GROUP
    inputs = hidden_in.astype(jnp.float32).reshape(group_count, GROUP, D)
    cotangents = out_grad.astype(jnp.float32).reshape(group_count, GROUP, D)
    seg_groups = segments.reshape(group_count, GROUP)

    def one_group(totals, pieces):
        group_in, group_cot, group_seg = pieces

        def forward(params, values):
            return layer(params, values, group_seg)
        result, pullback = jax.vjp(forward, weights, group_in)
        param_grads, input_grad = pullback(group_cot)
        return (jax.tree.map(jnp.add, totals, param_grads), (result, input_grad))
    starting = jax.tree.map(jnp.zeros_like, weights)
    totals, (results, input_grads) = lax.scan(one_group, starting, (inputs, cotangents, seg_groups))
    return (results.reshape(TOKENS, D).astype(jnp.bfloat16), input_grads.reshape(TOKENS, D), totals[0], totals[1], totals[2], totals[3], totals[4], totals[5], totals[6], totals[7], totals[8], totals[9], totals[10], totals[11], totals[12], totals[13], totals[14], totals[15], totals[16], totals[17], totals[18], totals[19])
```

```python
import functools
import jax
import jax.numpy as jnp
from jax import lax
from jax.experimental import pallas as pl
from jax.experimental.pallas import tpu as pltpu
from jax.sharding import PartitionSpec as P

STATE = 16
BLOCK = 16
CHUNK = 128


def dot_nn(left, right):
    return lax.dot_general(left, right, (((1,), (0,)), ((), ())), preferred_element_type=jnp.float32)


def dot_tn(left, right):
    return lax.dot_general(left, right, (((0,), (0,)), ((), ())), preferred_element_type=jnp.float32)


def dot_nt(left, right):
    return lax.dot_general(left, right, (((1,), (1,)), ((), ())), preferred_element_type=jnp.float32)


def sigmoid(values):
    return 1.0 / (1.0 + jnp.exp(-values))


def softplus(values):
    return jnp.maximum(values, 0.0) + jnp.log(1.0 + jnp.exp(-jnp.abs(values)))


def scan_forward_kernel(
    inner_ref, gate_ref, bcd_ref, eb_ref, ec_ref, mask_ref, param_ref, step_ref,
    gated_ref, conv_ref, mixed_ref, start_ref,
    shifted, decay, drive, spread, states, scanned, carry,
):
    chunk = inner_ref.shape[0]

    @pl.when(pl.program_id(0) == 0)
    def _():
        carry[...] = jnp.zeros_like(carry)
        shifted[0:8, :] = jnp.zeros_like(shifted[0:8, :])

    x = inner_ref[...]
    shifted[8 : 8 + chunk, :] = x
    conv = param_ref[0:1, :] * x
    for lag in range(1, 4):
        conv += param_ref[lag : lag + 1, :] * (
            mask_ref[:, lag : lag + 1] * shifted[8 - lag : 8 - lag + chunk, :]
        )
    shifted[0:8, :] = x[chunk - 8 :, :]
    conv_ref[...] = conv
    driven = conv * sigmoid(conv)
    step = softplus(dot_nn(bcd_ref[...], step_ref[...]) + param_ref[4:5, :])
    decay[...] = jnp.exp(-step * param_ref[5:6, :]) * mask_ref[:, 0:1]
    drive[...] = (step * driven).astype(jnp.bfloat16)
    start_ref[0] = carry[...]

    def block(number, state):
        rows = pl.ds(pl.multiple_of(number * BLOCK, BLOCK), BLOCK)
        lanes = pl.ds(pl.multiple_of(number * 256, 256), 256)
        spread[...] = dot_tn(eb_ref[:, lanes], drive[rows, :])
        decays = decay[rows, :]
        for t in range(BLOCK):
            state = decays[t : t + 1, :] * state + spread[t * STATE : (t + 1) * STATE, :]
            states[t * STATE : (t + 1) * STATE, :] = state.astype(jnp.bfloat16)
        scanned[rows, :] = dot_nn(ec_ref[:, lanes], states[...])
        return state

    carry[...] = lax.fori_loop(0, chunk // BLOCK, block, carry[...])
    mixed = scanned[...] + param_ref[6:7, :] * driven
    mixed_ref[...] = mixed
    gate = gate_ref[...]
    gated_ref[...] = (mixed * gate * sigmoid(gate)).astype(jnp.bfloat16)


def scan_forward(inner, gate, bcd_low, eb, ec, masks, params, step_pad):
    length, channels = inner.shape
    chunk = min(CHUNK, length)
    row = lambda i: (i, 0)
    fixed = lambda i: (0, 0)
    return pl.pallas_call(
        scan_forward_kernel,
        grid=(length // chunk,),
        in_specs=[
            pl.BlockSpec((chunk, channels), row),
            pl.BlockSpec((chunk, channels), row),
            pl.BlockSpec((chunk, bcd_low.shape[1]), row),
            pl.BlockSpec((BLOCK, chunk * STATE), lambda i: (0, i)),
            pl.BlockSpec((BLOCK, chunk * STATE), lambda i: (0, i)),
            pl.BlockSpec((chunk, masks.shape[1]), row),
            pl.BlockSpec(params.shape, fixed),
            pl.BlockSpec(step_pad.shape, fixed),
        ],
        out_specs=[
            pl.BlockSpec((chunk, channels), row),
            pl.BlockSpec((chunk, channels), row),
            pl.BlockSpec((chunk, channels), row),
            pl.BlockSpec((1, STATE, channels), lambda i: (i, 0, 0)),
        ],
        out_shape=[
            jax.ShapeDtypeStruct((length, channels), jnp.bfloat16),
            jax.ShapeDtypeStruct((length, channels), jnp.float32),
            jax.ShapeDtypeStruct((length, channels), jnp.float32),
            jax.ShapeDtypeStruct((length // chunk, STATE, channels), jnp.float32),
        ],
        scratch_shapes=[
            pltpu.VMEM((chunk + 8, channels), jnp.float32),
            pltpu.VMEM((chunk, channels), jnp.float32),
            pltpu.VMEM((chunk, channels), jnp.bfloat16),
            pltpu.VMEM((BLOCK * STATE, channels), jnp.float32),
            pltpu.VMEM((BLOCK * STATE, channels), jnp.bfloat16),
            pltpu.VMEM((chunk, channels), jnp.float32),
            pltpu.VMEM((STATE, channels), jnp.float32),
        ],
        compiler_params=pltpu.CompilerParams(vmem_limit_bytes=48 * 2**20),
        cost_estimate=pl.CostEstimate(
            flops=length * channels * 600, bytes_accessed=length * channels * 20, transcendentals=length * channels * 5
        ),
        name="scan_forward",
    )(inner, gate, bcd_low, eb, ec, masks, params, step_pad)


def scan_backward_kernel(
    inner_ref, gate_ref, conv_ref, mixed_ref, up_ref, bcd_ref, eb_ref, ec_ref, mask_ref, param_ref,
    step_ref, start_ref,
    d_inner_ref, d_gate_ref, d_low_ref, db_ref, dc_ref, d_step_ref, d_param_ref,
    shifted, decay, drive, spread, states, upstream, grads, products, d_drive, d_decay, carry,
):
    chunk = inner_ref.shape[0]
    blocks = chunk // BLOCK

    @pl.when(pl.program_id(0) == 0)
    def _():
        carry[...] = jnp.zeros_like(carry)
        shifted[chunk : chunk + 8, :] = jnp.zeros_like(shifted[chunk : chunk + 8, :])
        d_step_ref[...] = jnp.zeros_like(d_step_ref)
        d_param_ref[...] = jnp.zeros_like(d_param_ref)

    conv = conv_ref[...]
    conv_sig = sigmoid(conv)
    driven = conv * conv_sig
    pre = dot_nn(bcd_ref[...], step_ref[...]) + param_ref[4:5, :]
    step = softplus(pre)
    decay[...] = jnp.exp(-step * param_ref[5:6, :]) * mask_ref[:, 0:1]
    drive[...] = (step * driven).astype(jnp.bfloat16)
    gate = gate_ref[...]
    gate_sig = sigmoid(gate)
    d_gated = up_ref[...].astype(jnp.float32)
    d_gate_ref[...] = (
        d_gated * mixed_ref[...] * gate_sig * (1.0 + gate * (1.0 - gate_sig))
    ).astype(jnp.bfloat16)
    d_mixed = d_gated * gate * gate_sig
    upstream[...] = d_mixed.astype(jnp.bfloat16)

    states[0:STATE, :] = start_ref[0].astype(jnp.bfloat16)

    def replay(number, state):
        rows = pl.ds(pl.multiple_of(number * BLOCK, BLOCK), BLOCK)
        lanes = pl.ds(pl.multiple_of(number * 256, 256), 256)
        spread[...] = dot_tn(eb_ref[:, lanes], drive[rows, :])
        decays = decay[rows, :]
        for t in range(BLOCK):
            state = decays[t : t + 1, :] * state + spread[t * STATE : (t + 1) * STATE, :]
            where = pl.multiple_of(number * 256 + (t + 1) * STATE, STATE)
            states[pl.ds(where, STATE), :] = state.astype(jnp.bfloat16)
        return state

    lax.fori_loop(0, blocks, replay, start_ref[0])

    own = (
        lax.broadcasted_iota(jnp.int32, (BLOCK, 256), 1) // STATE
        == lax.broadcasted_iota(jnp.int32, (BLOCK, 256), 0)
    )
    ones = own.astype(jnp.bfloat16)

    def back(count, carried):
        number = blocks - 1 - count
        rows = pl.ds(pl.multiple_of(number * BLOCK, BLOCK), BLOCK)
        lanes = pl.ds(pl.multiple_of(number * 256, 256), 256)
        spread[...] = dot_tn(ec_ref[:, lanes], upstream[rows, :])
        decays = decay[rows, :]
        for t in reversed(range(BLOCK)):
            grad = carried + spread[t * STATE : (t + 1) * STATE, :]
            low = grad.astype(jnp.bfloat16)
            grads[t * STATE : (t + 1) * STATE, :] = low
            where = pl.multiple_of(number * 256 + t * STATE, STATE)
            products[t * STATE : (t + 1) * STATE, :] = low * states[pl.ds(where, STATE), :]
            carried = decays[t : t + 1, :] * grad
        d_drive[rows, :] = dot_nn(eb_ref[:, lanes], grads[...])
        d_decay[rows, :] = dot_nn(ones, products[...])
        after = states[pl.ds(pl.multiple_of(number * 256 + STATE, STATE), 256), :]
        dc_all = dot_nt(upstream[rows, :], after)
        db_all = dot_nt(drive[rows, :], grads[...])
        dc_ref[0, pl.ds(number, 1), :] = jnp.sum(jnp.where(own, dc_all, 0.0), axis=0, keepdims=True)
        db_ref[0, pl.ds(number, 1), :] = jnp.sum(jnp.where(own, db_all, 0.0), axis=0, keepdims=True)
        return carried

    carry[...] = lax.fori_loop(0, blocks, back, carry[...])

    d_rate = -d_decay[...] * decay[...]
    rate_scale = param_ref[5:6, :]
    d_pre = (d_drive[...] * driven + d_rate * rate_scale) * sigmoid(pre)
    d_pre_low = d_pre.astype(jnp.bfloat16)
    d_low_ref[...] = dot_nt(d_pre_low, step_ref[...])
    d_step_ref[...] += dot_tn(bcd_ref[...], d_pre_low)
    d_conv = (d_drive[...] * step + param_ref[6:7, :] * d_mixed) * conv_sig * (
        1.0 + conv * (1.0 - conv_sig)
    )
    x = inner_ref[...]
    shifted[0:chunk, :] = d_conv
    d_inner = param_ref[0:1, :] * d_conv
    d_param_ref[0:1, :] += jnp.sum(d_conv * x, axis=0, keepdims=True)
    for lag in range(1, 4):
        later = mask_ref[:, 3 + lag : 4 + lag] * shifted[lag : lag + chunk, :]
        d_inner += param_ref[lag : lag + 1, :] * later
        d_param_ref[lag : lag + 1, :] += jnp.sum(later * x, axis=0, keepdims=True)
    shifted[chunk : chunk + 8, :] = d_conv[0:8, :]
    d_inner_ref[...] = d_inner.astype(jnp.bfloat16)
    d_param_ref[4:5, :] += jnp.sum(d_pre, axis=0, keepdims=True)
    d_param_ref[5:6, :] += jnp.sum(d_rate * step, axis=0, keepdims=True) * rate_scale
    d_param_ref[6:7, :] += jnp.sum(d_mixed * driven, axis=0, keepdims=True)


def scan_backward(inner, gate, conv, mixed, d_gated, bcd_low, eb, ec, masks, params, step_pad, starts):
    length, channels = inner.shape
    chunk = min(CHUNK, length)
    count = length // chunk
    features = bcd_low.shape[1]
    row = lambda i: (count - 1 - i, 0)
    fixed = lambda i: (0, 0)
    wide = pl.BlockSpec((chunk, channels), row)
    flat = pl.BlockSpec((BLOCK, chunk * STATE), lambda i: (0, count - 1 - i))
    lists = pl.BlockSpec((1, chunk // BLOCK, 256), lambda i: (count - 1 - i, 0, 0))
    return pl.pallas_call(
        scan_backward_kernel,
        grid=(count,),
        in_specs=[
            wide, wide, wide, wide, wide,
            pl.BlockSpec((chunk, features), row),
            flat, flat,
            pl.BlockSpec((chunk, masks.shape[1]), row),
            pl.BlockSpec(params.shape, fixed),
            pl.BlockSpec(step_pad.shape, fixed),
            pl.BlockSpec((1, STATE, channels), lambda i: (count - 1 - i, 0, 0)),
        ],
        out_specs=[
            wide, wide,
            pl.BlockSpec((chunk, features), row),
            lists, lists,
            pl.BlockSpec((features, channels), fixed),
            pl.BlockSpec((8, channels), fixed),
        ],
        out_shape=[
            jax.ShapeDtypeStruct((length, channels), jnp.bfloat16),
            jax.ShapeDtypeStruct((length, channels), jnp.bfloat16),
            jax.ShapeDtypeStruct((length, features), jnp.float32),
            jax.ShapeDtypeStruct((count, chunk // BLOCK, 256), jnp.float32),
            jax.ShapeDtypeStruct((count, chunk // BLOCK, 256), jnp.float32),
            jax.ShapeDtypeStruct((features, channels), jnp.float32),
            jax.ShapeDtypeStruct((8, channels), jnp.float32),
        ],
        scratch_shapes=[
            pltpu.VMEM((chunk + 8, channels), jnp.float32),
            pltpu.VMEM((chunk, channels), jnp.float32),
            pltpu.VMEM((chunk, channels), jnp.bfloat16),
            pltpu.VMEM((BLOCK * STATE, channels), jnp.float32),
            pltpu.VMEM(((chunk + 1) * STATE, channels), jnp.bfloat16),
            pltpu.VMEM((chunk, channels), jnp.bfloat16),
            pltpu.VMEM((BLOCK * STATE, channels), jnp.bfloat16),
            pltpu.VMEM((BLOCK * STATE, channels), jnp.bfloat16),
            pltpu.VMEM((chunk, channels), jnp.float32),
            pltpu.VMEM((chunk, channels), jnp.float32),
            pltpu.VMEM((STATE, channels), jnp.float32),
        ],
        compiler_params=pltpu.CompilerParams(vmem_limit_bytes=48 * 2**20),
        cost_estimate=pl.CostEstimate(
            flops=length * channels * 1600, bytes_accessed=length * channels * 26, transcendentals=length * channels * 8
        ),
        name="scan_backward",
    )(inner, gate, conv, mixed, d_gated, bcd_low, eb, ec, masks, params, step_pad, starts)


def spread_rows(values):
    length = values.shape[0]
    token = jnp.arange(length * STATE, dtype=jnp.int32) // STATE
    own = (token[None, :] % BLOCK) == jnp.arange(BLOCK, dtype=jnp.int32)[:, None]
    return jnp.where(own, values.reshape(1, length * STATE), 0.0).astype(jnp.bfloat16)


def scan_masks(segments):
    length = segments.shape[0]
    columns = []
    for lag in (1, 1, 2, 3):
        before = jnp.concatenate([jnp.full((lag,), -1, jnp.int32), segments[:-lag]])
        columns.append(before == segments)
    for lag in (1, 2, 3):
        after = jnp.concatenate([segments[lag:], jnp.full((lag,), -1, jnp.int32)])
        columns.append(after == segments)
    columns.append(jnp.zeros((length,), bool))
    return jnp.stack(columns, axis=1).astype(jnp.float32)


HEAD_DIM = 64
WINDOW = 1024

epsilon = 1e-05

EVEN_ORDER = (0, 4, 2, 6, 1, 3, 5, 7)
ODD_ORDER = (0, 2, 4, 6, 1, 5, 3, 7)


def inverse_rms(values):
    return lax.rsqrt(jnp.mean(values * values, axis=-1, keepdims=True) + epsilon)


def norm_backward(values, inv_scale, gain_vec, upstream):
    weighted = upstream * gain_vec
    d_values = inv_scale * weighted - values * inv_scale**3 * jnp.mean(
        values * weighted, axis=-1, keepdims=True
    )
    return (d_values, jnp.sum(upstream * values * inv_scale, axis=0))


def contract(pattern, left_side, right_side):
    return jnp.einsum(pattern, left_side, right_side, preferred_element_type=jnp.float32)


def low(values):
    return values.astype(jnp.bfloat16)


def hop_first(shard):
    return lax.ppermute(shard, "dp", [(i, i ^ (2 if i & 1 else 4)) for i in range(8)])


def hop_second(shard):
    return lax.ppermute(shard, "dp", [(i, i ^ (4 if i & 1 else 2)) for i in range(8)])


def hop_core(shard):
    return lax.ppermute(shard, "dp", [(i, i ^ 1) for i in range(8)])


def gather_rows(shard):
    axis = shard.ndim - 2
    if lax.axis_size("dp") != 8:
        return lax.all_gather(shard, "dp", axis=axis, tiled=True)
    first = hop_first(shard)
    second = hop_second(shard)
    third = hop_second(first)
    mine = [shard, first, second, third]
    return jnp.concatenate(mine + [hop_core(piece) for piece in mine], axis)


def scatter_rows(total):
    axis = total.ndim - 2
    if lax.axis_size("dp") != 8:
        return lax.psum_scatter(
            total, "dp", scatter_dimension=axis, tiled=True
        ).astype(jnp.float32)
    size = total.shape[axis] // 8

    def part(values, begin, end):
        return lax.slice_in_dim(values, begin * size, end * size, axis=axis)

    def wide(values, begin, end):
        return part(values, begin, end).astype(jnp.float32)

    other = hop_core(part(total, 4, 8))
    across = hop_second(low(wide(total, 2, 4) + wide(other, 2, 4)))
    near = hop_first(low(wide(total, 1, 2) + wide(other, 1, 2) + wide(across, 1, 2)))
    return (
        wide(total, 0, 1) + wide(other, 0, 1) + wide(across, 0, 1) + near.astype(jnp.float32)
    )


def order_matrix(width):
    if lax.axis_size("dp") != 8:
        return None
    rank = lax.axis_index("dp").astype(jnp.int32)
    size = width // 8
    column = jnp.arange(width, dtype=jnp.int32)
    even = jnp.repeat(jnp.array(EVEN_ORDER, jnp.int32), size)
    odd = jnp.repeat(jnp.array(ODD_ORDER, jnp.int32), size)
    source = (rank ^ jnp.where(rank & 1 == 1, odd, even)) * size + column % size
    return (column[:, None] == source[None, :]).astype(jnp.bfloat16)


def to_order(values, order):
    return values if order is None else low(jnp.dot(values, order))


def from_order(values, order):
    return values if order is None else low(contract("ta,ba->tb", values, order))


def shards(
    hidden_in,
    out_grad,
    segments,
    norm_input,
    query_weight,
    key_weight,
    value_weight,
    attn_out_weight,
    norm_attn,
    ssm_x_weight,
    ssm_gate_weight,
    ssm_bcd_weight,
    step_weight,
    step_bias,
    decay_log,
    skip_gain,
    conv_weight,
    ssm_out_weight,
    norm_ssm,
    norm_ffn,
    gate_weight,
    up_weight,
    down_weight,
):
    tokens, width = hidden_in.shape
    data_ways = lax.axis_size("dp")
    tensor_ways = lax.axis_size("tensor")
    tensor_rank = lax.axis_index("tensor")
    channels = ssm_x_weight.shape[1]
    rank_rows = step_weight.shape[0]
    taps = conv_weight.shape[0]
    owned = step_weight.shape[1]
    spans = channels // owned
    group = segments.shape[0]

    order = order_matrix(width)

    small = jnp.concatenate(
        [step_weight, step_bias[None], decay_log[None], skip_gain[None], conv_weight], axis=0
    )
    small_rows = small.shape[0]
    gains = jnp.stack([norm_input, norm_attn, norm_ssm, norm_ffn])
    small_all = lax.all_gather(small, "dp", axis=0)
    gains_all = lax.all_gather(gains, "dp", axis=1, tiled=True).astype(jnp.float32)
    gain_input, gain_attn, gain_ssm, gain_ffn = (gains_all[i] for i in range(4))
    small_local = lax.dynamic_slice_in_dim(small_all, tensor_rank * spans, spans, 0)
    small_local = small_local.transpose(1, 0, 2).reshape(small_rows, channels)
    step_local = small_local[:rank_rows]
    small_f32 = small_local[rank_rows:].astype(jnp.float32)
    bias_local, decay_local, skip_local, conv_local = (
        small_f32[0],
        small_f32[1],
        small_f32[2],
        small_f32[3:],
    )

    x_all = gather_rows(ssm_x_weight)
    ssm_gate_all = gather_rows(ssm_gate_weight)
    bcd_all = gather_rows(ssm_bcd_weight)
    query_all = gather_rows(query_weight)
    key_all = gather_rows(key_weight)
    value_all = gather_rows(value_weight)
    ssm_out_all = gather_rows(ssm_out_weight.T)
    attn_out_all = gather_rows(attn_out_weight)
    gate_all = gather_rows(gate_weight)
    up_all = gather_rows(up_weight)
    down_all = gather_rows(down_weight.T)

    input_f32 = hidden_in.astype(jnp.float32)
    scale_in = inverse_rms(input_f32)
    normed = to_order(low(input_f32 * scale_in * gain_input), order)
    all_normed = lax.all_gather(normed, "tensor", axis=0, tiled=True)
    all_out_grad = lax.all_gather(to_order(out_grad, order), "tensor", axis=0, tiled=True)
    queries = low(jnp.dot(normed, query_all, preferred_element_type=jnp.float32))
    keys = low(jnp.dot(all_normed, key_all, preferred_element_type=jnp.float32))
    values = low(jnp.dot(all_normed, value_all, preferred_element_type=jnp.float32))
    inner_in = jnp.dot(all_normed, x_all, preferred_element_type=jnp.float32)
    gate_in = jnp.dot(all_normed, ssm_gate_all, preferred_element_type=jnp.float32)
    bcd_values = jnp.dot(all_normed, bcd_all, preferred_element_type=jnp.float32)

    bcd_low = low(bcd_values)
    spread_in = spread_rows(bcd_values[:, :STATE])
    spread_out = spread_rows(bcd_values[:, STATE : 2 * STATE])
    masks = scan_masks(segments)
    params = jnp.concatenate(
        [
            conv_local,
            bias_local[None],
            jnp.exp(decay_local)[None],
            skip_local[None],
            jnp.zeros((1, channels), jnp.float32),
        ]
    )
    step_pad = jnp.concatenate([jnp.zeros((2 * STATE, channels), jnp.bfloat16), step_local])
    gated_low, conv_total, mixed_total, starts = scan_forward(
        inner_in, gate_in, bcd_low, spread_in, spread_out, masks, params, step_pad
    )
    ssm_proj = lax.psum_scatter(
        low(contract("gc,dc->gd", gated_low, ssm_out_all)),
        "tensor",
        scatter_dimension=0,
        tiled=True,
    )
    ssm_proj = from_order(ssm_proj, order).astype(jnp.float32)

    query_pos = tensor_rank * tokens + jnp.arange(tokens, dtype=jnp.int32)
    key_pos = jnp.arange(group, dtype=jnp.int32)
    query_seg = lax.dynamic_slice_in_dim(segments, tensor_rank * tokens, tokens, 0)
    allowed = (
        (key_pos[None, :] <= query_pos[:, None])
        & (query_pos[:, None] - key_pos[None, :] < WINDOW)
        & (segments[None, :] == query_seg[:, None])
    )
    kv_groups = keys.shape[1] // HEAD_DIM
    repeat = queries.shape[1] // keys.shape[1]
    factor = HEAD_DIM ** (-0.5)
    query_groups = queries.reshape(tokens, kv_groups, repeat, HEAD_DIM).transpose(1, 0, 2, 3)
    key_groups = keys.reshape(group, kv_groups, HEAD_DIM).transpose(1, 0, 2)
    value_groups = values.reshape(group, kv_groups, HEAD_DIM).transpose(1, 0, 2)

    def masked_scores(query_g, key_g):
        raw_scores = contract("qrd,kd->rqk", query_g, key_g) * factor
        return jnp.where(allowed[None], raw_scores, -jnp.inf)

    def attend_group(pieces):
        query_g, key_g, value_g = pieces
        scores = masked_scores(query_g, key_g)
        row_peak = jnp.max(scores, axis=-1, keepdims=True)
        exponents = jnp.exp(scores - row_peak)
        row_total = jnp.sum(exponents, axis=-1, keepdims=True)
        probs_low = low(exponents / row_total)
        mixed = low(contract("rqk,kd->qrd", probs_low, value_g))
        return (mixed, row_peak + jnp.log(row_total))

    mixed_groups, log_totals = lax.map(attend_group, (query_groups, key_groups, value_groups))
    attended = to_order(mixed_groups.transpose(1, 0, 2, 3).reshape(tokens, -1), order)
    attn_proj = jnp.dot(attended, attn_out_all, preferred_element_type=jnp.float32)
    scale_attn = inverse_rms(attn_proj)

    scale_ssm = inverse_rms(ssm_proj)
    residual = input_f32 + 0.5 * (
        attn_proj * scale_attn * gain_attn + ssm_proj * scale_ssm * gain_ssm
    )
    scale_ffn = inverse_rms(residual)
    ffn_in = to_order(low(residual * scale_ffn * gain_ffn), order)
    all_ffn_in = lax.all_gather(ffn_in, "tensor", axis=0, tiled=True)
    gate_pre = jnp.dot(all_ffn_in, gate_all, preferred_element_type=jnp.float32)
    up_pre = jnp.dot(all_ffn_in, up_all, preferred_element_type=jnp.float32)
    sigmoid_gate = jax.nn.sigmoid(gate_pre)
    silu_gate = gate_pre * sigmoid_gate
    activated = low(silu_gate * up_pre)
    d_act = contract("gd,df->gf", all_out_grad, down_all)
    d_gate = low(d_act * up_pre * sigmoid_gate * (1.0 + gate_pre * (1.0 - sigmoid_gate)))
    d_up = low(d_act * silu_gate)
    d_ffn_part = contract("gf,df->gd", d_gate, gate_all) + contract("gf,df->gd", d_up, up_all)
    d_ffn_in = lax.psum_scatter(low(d_ffn_part), "tensor", scatter_dimension=0, tiled=True)
    d_ffn_in = from_order(d_ffn_in, order).astype(jnp.float32)
    ffn_out = lax.psum_scatter(
        low(contract("gf,df->gd", activated, down_all)),
        "tensor",
        scatter_dimension=0,
        tiled=True,
    )
    layer_out = low(residual + from_order(ffn_out, order).astype(jnp.float32))
    grad_gate = scatter_rows(low(contract("gd,gf->df", all_ffn_in, d_gate)))
    grad_up = scatter_rows(low(contract("gd,gf->df", all_ffn_in, d_up)))
    grad_down = scatter_rows(low(contract("gd,gf->df", all_out_grad, activated))).T

    d_res_norm, grad_gain_ffn = norm_backward(residual, scale_ffn, gain_ffn, d_ffn_in)
    d_residual = out_grad.astype(jnp.float32) + d_res_norm
    d_attn_proj, grad_gain_attn = norm_backward(attn_proj, scale_attn, gain_attn, 0.5 * d_residual)
    d_ssm_proj, grad_gain_ssm = norm_backward(ssm_proj, scale_ssm, gain_ssm, 0.5 * d_residual)
    d_attn_low = low(d_attn_proj)
    all_ssm_grad = lax.all_gather(to_order(low(d_ssm_proj), order), "tensor", axis=0, tiled=True)

    grad_attn_out = scatter_rows(low(contract("tc,td->cd", attended, d_attn_low)))
    d_attended = from_order(low(contract("td,cd->tc", d_attn_low, attn_out_all)), order)
    d_attended_groups = d_attended.reshape(tokens, kv_groups, repeat, HEAD_DIM).transpose(
        1, 0, 2, 3
    )

    def attend_back(pieces):
        query_g, key_g, value_g, d_mixed, log_g = pieces
        probs_again = jnp.exp(masked_scores(query_g, key_g) - log_g)
        d_probs = contract("qrd,kd->rqk", d_mixed, value_g)
        d_scores = low(
            probs_again * (d_probs - jnp.sum(probs_again * d_probs, axis=-1, keepdims=True))
        )
        d_query = low(contract("rqk,kd->qrd", d_scores, key_g) * factor)
        d_key = low(contract("rqk,qrd->kd", d_scores, query_g) * factor)
        d_value = low(contract("rqk,qrd->kd", low(probs_again), d_mixed))
        return (d_query, d_key, d_value)

    d_query_groups, d_key_groups, d_value_groups = lax.map(
        attend_back, (query_groups, key_groups, value_groups, d_attended_groups, log_totals)
    )
    d_queries = d_query_groups.transpose(1, 0, 2, 3).reshape(tokens, -1)
    d_keys = d_key_groups.transpose(1, 0, 2).reshape(group, -1)
    d_values = d_value_groups.transpose(1, 0, 2).reshape(group, -1)
    grad_query = scatter_rows(low(contract("td,te->de", normed, d_queries)))
    grad_key = scatter_rows(low(contract("td,te->de", all_normed, d_keys)))
    grad_value = scatter_rows(low(contract("td,te->de", all_normed, d_values)))
    d_normed_own = contract("te,de->td", d_queries, query_all)

    grad_ssm_out = scatter_rows(low(contract("gd,gc->dc", all_ssm_grad, gated_low))).T
    d_gated = contract("gd,dc->gc", all_ssm_grad, ssm_out_all)
    d_inner, d_gate_in, d_low, d_in_map, d_out_map, d_step_pad, d_params = scan_backward(
        inner_in,
        gate_in,
        conv_total,
        mixed_total,
        d_gated,
        bcd_low,
        spread_in,
        spread_out,
        masks,
        params,
        step_pad,
        starts,
    )
    d_bcd = low(
        jnp.concatenate(
            [
                d_in_map.reshape(group, STATE),
                d_out_map.reshape(group, STATE),
                d_low[:, 2 * STATE :],
            ],
            axis=1,
        )
    )
    d_normed_part = (
        contract("gc,dc->gd", d_inner, x_all)
        + contract("gc,dc->gd", d_gate_in, ssm_gate_all)
        + contract("gc,dc->gd", d_bcd, bcd_all)
        + contract("gc,dc->gd", d_keys, key_all)
        + contract("gc,dc->gd", d_values, value_all)
    )
    d_normed_sum = lax.psum_scatter(
        low(d_normed_part), "tensor", scatter_dimension=0, tiled=True
    ).astype(jnp.float32)
    d_normed = from_order(low(d_normed_sum + d_normed_own), order).astype(jnp.float32)
    grad_x = scatter_rows(low(contract("gd,gc->dc", all_normed, d_inner)))
    grad_ssm_gate = scatter_rows(low(contract("gd,gc->dc", all_normed, d_gate_in)))
    grad_bcd = scatter_rows(low(contract("gd,gc->dc", all_normed, d_bcd)))
    d_input_norm, grad_gain_input = norm_backward(input_f32, scale_in, gain_input, d_normed)
    grad_input = d_residual + d_input_norm

    d_small = jnp.concatenate(
        [d_step_pad[2 * STATE :], d_params[4:7], d_params[:taps]], axis=0
    )
    d_small = d_small.reshape(small_rows, spans, owned).transpose(1, 0, 2)
    d_small_all = lax.dynamic_update_slice_in_dim(
        jnp.zeros((data_ways, small_rows, owned), jnp.bfloat16),
        low(d_small),
        tensor_rank * spans,
        0,
    )
    d_small_own = lax.psum_scatter(d_small_all, "dp", scatter_dimension=0, tiled=True)
    d_small_own = lax.psum(d_small_own, "tensor")[0].astype(jnp.float32)
    d_gains = low(jnp.stack([grad_gain_input, grad_gain_attn, grad_gain_ssm, grad_gain_ffn]))
    d_gains = lax.psum(d_gains, ("dp", "tensor")).astype(jnp.float32)
    d_gains = lax.dynamic_slice_in_dim(
        d_gains, lax.axis_index("dp") * (width // data_ways), width // data_ways, 1
    )

    def over_tensor(values):
        return lax.psum(low(values), "tensor").astype(jnp.float32)

    return (
        layer_out,
        grad_input,
        d_gains[0],
        over_tensor(grad_query),
        over_tensor(grad_key),
        over_tensor(grad_value),
        over_tensor(grad_attn_out),
        d_gains[1],
        grad_x,
        grad_ssm_gate,
        over_tensor(grad_bcd),
        d_small_own[:rank_rows],
        d_small_own[rank_rows],
        d_small_own[rank_rows + 1],
        d_small_own[rank_rows + 2],
        d_small_own[rank_rows + 3 :],
        grad_ssm_out,
        d_gains[2],
        d_gains[3],
        grad_gate,
        grad_up,
        grad_down,
    )


def solution(mesh):
    rows = P(("dp", "tensor"), None)
    both = P("dp", "tensor")
    in_specs = (
        rows,
        rows,
        P("dp"),
        P("dp"),
        P("dp", None),
        P("dp", None),
        P("dp", None),
        P("dp", None),
        P("dp"),
        both,
        both,
        P("dp", None),
        P(None, "dp"),
        P("dp"),
        P("dp"),
        P("dp"),
        P(None, "dp"),
        P("tensor", "dp"),
        P("dp"),
        P("dp"),
        both,
        both,
        P("tensor", "dp"),
    )
    out_specs = (
        rows,
        rows,
        P("dp"),
        P("dp", None),
        P("dp", None),
        P("dp", None),
        P("dp", None),
        P("dp"),
        both,
        both,
        P("dp", None),
        P(None, "dp"),
        P("dp"),
        P("dp"),
        P("dp"),
        P(None, "dp"),
        P("tensor", "dp"),
        P("dp"),
        P("dp"),
        both,
        both,
        P("tensor", "dp"),
    )
    return jax.shard_map(shards, mesh=mesh, in_specs=in_specs, out_specs=out_specs, check_vma=False)
```

```python
import functools

import jax
import jax.numpy as jnp
from jax import lax
from jax.experimental import pallas as pl
from jax.experimental.pallas import tpu as pltpu
from jax.sharding import PartitionSpec as P

STATE = 16
BLOCK = 16
CHUNK = 128
HEAD_DIM = 64
WINDOW = 1024

epsilon = 1e-05

VMEM_LIMIT = 58 * 2**20

EVEN_ORDER = (0, 4, 2, 6, 1, 3, 5, 7)
ODD_ORDER = (0, 2, 4, 6, 1, 5, 3, 7)


def dot_nn(left, right):
    return lax.dot_general(left, right, (((1,), (0,)), ((), ())), preferred_element_type=jnp.float32)


def dot_tn(left, right):
    return lax.dot_general(left, right, (((0,), (0,)), ((), ())), preferred_element_type=jnp.float32)


def dot_nt(left, right):
    return lax.dot_general(left, right, (((1,), (1,)), ((), ())), preferred_element_type=jnp.float32)


def sigmoid(values):
    return 1.0 / (1.0 + jnp.exp(-values))


def softplus(values):
    return jnp.maximum(values, 0.0) + jnp.log(1.0 + jnp.exp(-jnp.abs(values)))


def scan_forward_kernel(
    x_ref, gain_ref, inner_w, gate_w, bcd_w, out_w, step_w, param_ref, mask_ref, pick_in, pick_out,
    carry_in, tail_in, *rest,
):
    (
        normed_ref, inner_ref, gate_ref, bcd_ref, conv_ref, mixed_ref, gated_ref, start_ref, states,
        part_ref, carry_out, tail_out,
    ) = rest[-20:-8]
    shifted, decay, drive, spread_in, spread_out, spread, scanned, carry = rest[-8:]
    chunk = x_ref.shape[0]

    @pl.when(pl.program_id(0) == 0)
    def _():
        carry[...] = carry_in[...]
        shifted[0:8, :] = tail_in[...]

    row = x_ref[...].astype(jnp.float32)
    scale = lax.rsqrt(jnp.mean(row * row, axis=-1, keepdims=True) + epsilon)
    normed = (row * scale * gain_ref[...]).astype(jnp.bfloat16)
    normed_ref[...] = normed
    x = dot_nn(normed, inner_w[...])
    inner_ref[...] = x
    bcd = dot_nn(normed, bcd_w[...]).astype(jnp.bfloat16)
    bcd_ref[...] = bcd
    own = own_lanes(chunk)
    spread_in[...] = jnp.where(own, dot_nn(bcd, pick_in[...]), 0.0).astype(jnp.bfloat16)
    spread_out[...] = jnp.where(own, dot_nn(bcd, pick_out[...]), 0.0).astype(jnp.bfloat16)
    shifted[8 : 8 + chunk, :] = x
    conv = param_ref[0:1, :] * x
    for lag in range(1, 4):
        conv += param_ref[lag : lag + 1, :] * (
            mask_ref[:, lag : lag + 1] * shifted[8 - lag : 8 - lag + chunk, :]
        )
    shifted[0:8, :] = x[chunk - 8 :, :]
    tail_out[...] = x[chunk - 8 :, :]
    conv_ref[...] = conv
    driven = conv * sigmoid(conv)
    step = softplus(dot_nn(bcd, step_w[...]) + param_ref[4:5, :])
    decay[...] = jnp.exp(-step * param_ref[5:6, :]) * mask_ref[:, 0:1]
    drive[...] = (step * driven).astype(jnp.bfloat16)
    start_ref[0] = carry[...].astype(jnp.bfloat16)

    def block(number, state):
        rows = pl.ds(pl.multiple_of(number * BLOCK, BLOCK), BLOCK)
        wide = pl.ds(pl.multiple_of(number * 256, 256), 256)
        spread[...] = dot_tn(spread_in[rows, :], drive[rows, :])
        decays = decay[rows, :]
        for t in range(BLOCK):
            state = decays[t : t + 1, :] * state + spread[t * STATE : (t + 1) * STATE, :]
            where = pl.multiple_of(number * 256 + t * STATE, STATE)
            states[pl.ds(where, STATE), :] = state.astype(jnp.bfloat16)
        scanned[rows, :] = dot_nn(spread_out[rows, :], states[wide, :])
        return state

    carry[...] = lax.fori_loop(0, chunk // BLOCK, block, carry[...])
    carry_out[...] = carry[...]
    mixed = scanned[...] + param_ref[6:7, :] * driven
    mixed_ref[...] = mixed
    gate = dot_nn(normed, gate_w[...])
    gate_ref[...] = gate
    gated = (mixed * gate * sigmoid(gate)).astype(jnp.bfloat16)
    gated_ref[...] = gated
    part_ref[...] = dot_nt(gated, out_w[...]).astype(jnp.bfloat16)


def own_lanes(chunk):
    return (
        lax.broadcasted_iota(jnp.int32, (chunk, 256), 1) // STATE
        == lax.broadcasted_iota(jnp.int32, (chunk, 256), 0) % BLOCK
    )


def picks(features, begin):
    row = jnp.arange(features, dtype=jnp.int32)[:, None]
    lane = jnp.arange(256, dtype=jnp.int32)[None, :]
    return (row == begin + lane % STATE).astype(jnp.bfloat16)


def whole(array):
    return pl.BlockSpec(array.shape, lambda i: (0, 0), pipeline_mode=pl.Buffered(1))


def scan_forward(x, gain, inner_w, gate_w, bcd_w, out_w, step_w, params, masks, begin, end, earlier=None):
    length, width = x.shape
    channels = inner_w.shape[1]
    features = bcd_w.shape[1]
    chunk = min(CHUNK, length)
    row = lambda i: (begin + i, 0)
    pick_in, pick_out = picks(features, 0), picks(features, STATE)
    fixed = [gain, inner_w, gate_w, bcd_w, out_w, step_w, params]
    tall = pl.BlockSpec((chunk, channels), row)
    if earlier is None:
        state_in = [jnp.zeros((STATE, channels), jnp.float32), jnp.zeros((8, channels), jnp.float32)]
        filled = []
    else:
        state_in = list(earlier[10:])
        filled = list(earlier[:10])
    inputs = [x, *fixed, masks, pick_in, pick_out, *state_in]
    return pl.pallas_call(
        scan_forward_kernel,
        grid=(end - begin,),
        in_specs=[pl.BlockSpec((chunk, width), row)]
        + [whole(v) for v in fixed]
        + [pl.BlockSpec((chunk, masks.shape[1]), row), whole(pick_in), whole(pick_out)]
        + [whole(v) for v in state_in]
        + [pl.BlockSpec(memory_space=pl.ANY)] * len(filled),
        out_specs=[
            pl.BlockSpec((chunk, width), row),
            tall,
            tall,
            pl.BlockSpec((chunk, features), row),
            tall,
            tall,
            tall,
            pl.BlockSpec((1, STATE, channels), lambda i: (begin + i, 0, 0)),
            pl.BlockSpec((chunk * STATE, channels), row),
            pl.BlockSpec((chunk, width), row),
            pl.BlockSpec((STATE, channels), lambda i: (0, 0)),
            pl.BlockSpec((8, channels), lambda i: (0, 0)),
        ],
        out_shape=[
            jax.ShapeDtypeStruct((length, width), jnp.bfloat16),
            jax.ShapeDtypeStruct((length, channels), jnp.float32),
            jax.ShapeDtypeStruct((length, channels), jnp.float32),
            jax.ShapeDtypeStruct((length, features), jnp.bfloat16),
            jax.ShapeDtypeStruct((length, channels), jnp.float32),
            jax.ShapeDtypeStruct((length, channels), jnp.float32),
            jax.ShapeDtypeStruct((length, channels), jnp.bfloat16),
            jax.ShapeDtypeStruct((length // chunk, STATE, channels), jnp.bfloat16),
            jax.ShapeDtypeStruct((length * STATE, channels), jnp.bfloat16),
            jax.ShapeDtypeStruct((length, width), jnp.bfloat16),
            jax.ShapeDtypeStruct((STATE, channels), jnp.float32),
            jax.ShapeDtypeStruct((8, channels), jnp.float32),
        ],
        input_output_aliases={len(inputs) + i: i for i in range(len(filled))},
        scratch_shapes=[
            pltpu.VMEM((chunk + 8, channels), jnp.float32),
            pltpu.VMEM((chunk, channels), jnp.float32),
            pltpu.VMEM((chunk, channels), jnp.bfloat16),
            pltpu.VMEM((chunk, 256), jnp.bfloat16),
            pltpu.VMEM((chunk, 256), jnp.bfloat16),
            pltpu.VMEM((BLOCK * STATE, channels), jnp.float32),
            pltpu.VMEM((chunk, channels), jnp.float32),
            pltpu.VMEM((STATE, channels), jnp.float32),
        ],
        compiler_params=pltpu.CompilerParams(vmem_limit_bytes=VMEM_LIMIT),
        cost_estimate=pl.CostEstimate(
            flops=length * channels * 80000 * (end - begin) * chunk // length,
            bytes_accessed=length * channels * 30,
            transcendentals=length * channels * 5,
        ),
        name="scan_forward",
    )(*inputs, *filled)


def scan_backward_kernel(
    normed_up_ref, inner_ref, gate_ref, bcd_ref, conv_ref, mixed_ref, addend_ref,
    inner_w, gate_w, bcd_w, out_w, step_w, param_ref, mask_ref, pick_in, pick_out, start_ref, states,
    carry_in, tail_in, d_step_in, d_param_in, *rest,
):
    (
        d_inner_ref, d_gate_ref, d_bcd_ref, part_ref, d_step_ref, d_param_ref, carry_out, tail_out,
    ) = rest[-20:-12]
    (
        shifted, decay, drive, spread_in, spread_out, spread, upstream, grads, products, d_drive,
        d_decay, carry,
    ) = rest[-12:]
    chunk = inner_ref.shape[0]
    blocks = chunk // BLOCK

    @pl.when(pl.program_id(0) == 0)
    def _():
        carry[...] = carry_in[...]
        shifted[chunk : chunk + 8, :] = tail_in[...]
        d_step_ref[...] = d_step_in[...]
        d_param_ref[...] = d_param_in[...]

    conv = conv_ref[...]
    conv_sig = sigmoid(conv)
    driven = conv * conv_sig
    bcd = bcd_ref[...]
    all_lanes = own_lanes(chunk)
    spread_in[...] = jnp.where(all_lanes, dot_nn(bcd, pick_in[...]), 0.0).astype(jnp.bfloat16)
    spread_out[...] = jnp.where(all_lanes, dot_nn(bcd, pick_out[...]), 0.0).astype(jnp.bfloat16)
    pre = dot_nn(bcd, step_w[...]) + param_ref[4:5, :]
    step = softplus(pre)
    decay[...] = jnp.exp(-step * param_ref[5:6, :]) * mask_ref[:, 0:1]
    drive[...] = (step * driven).astype(jnp.bfloat16)
    gate = gate_ref[...]
    gate_sig = sigmoid(gate)
    d_gated = dot_nn(normed_up_ref[...], out_w[...])
    d_gate = (d_gated * mixed_ref[...] * gate_sig * (1.0 + gate * (1.0 - gate_sig))).astype(jnp.bfloat16)
    d_gate_ref[...] = d_gate
    d_mixed = d_gated * gate * gate_sig
    upstream[...] = d_mixed.astype(jnp.bfloat16)

    own = own_lanes(BLOCK)
    ones = own.astype(jnp.bfloat16)

    def back(count, carried):
        number = blocks - 1 - count
        rows = pl.ds(pl.multiple_of(number * BLOCK, BLOCK), BLOCK)
        wide = pl.ds(pl.multiple_of(number * 256, 256), 256)
        spread[...] = dot_tn(spread_out[rows, :], upstream[rows, :])
        decays = decay[rows, :]
        ahead = pl.multiple_of(jnp.maximum(number * 256 - STATE, 0), STATE)
        entering = jnp.where(number == 0, start_ref[0], states[pl.ds(ahead, STATE), :])
        for t in reversed(range(BLOCK)):
            grad = carried + spread[t * STATE : (t + 1) * STATE, :]
            low = grad.astype(jnp.bfloat16)
            grads[t * STATE : (t + 1) * STATE, :] = low
            if t:
                where = pl.multiple_of(number * 256 + (t - 1) * STATE, STATE)
                before = states[pl.ds(where, STATE), :]
            else:
                before = entering
            products[t * STATE : (t + 1) * STATE, :] = low * before
            carried = decays[t : t + 1, :] * grad
        d_drive[rows, :] = dot_nn(spread_in[rows, :], grads[...])
        d_decay[rows, :] = dot_nn(ones, products[...])
        d_out = jnp.where(own, dot_nt(upstream[rows, :], states[wide, :]), 0.0).astype(jnp.bfloat16)
        d_in = jnp.where(own, dot_nt(drive[rows, :], grads[...]), 0.0).astype(jnp.bfloat16)
        spread_out[rows, :] = d_out
        spread_in[rows, :] = d_in
        return carried

    carry[...] = lax.fori_loop(0, blocks, back, carry[...])

    d_rate = -d_decay[...] * decay[...]
    rate_scale = param_ref[5:6, :]
    d_pre = (d_drive[...] * driven + d_rate * rate_scale) * sigmoid(pre)
    d_pre_low = d_pre.astype(jnp.bfloat16)
    d_bcd = (
        dot_nt(d_pre_low, step_w[...])
        + dot_nt(spread_out[...], pick_out[...])
        + dot_nt(spread_in[...], pick_in[...])
    ).astype(jnp.bfloat16)
    d_bcd_ref[...] = d_bcd
    d_step_ref[...] += dot_tn(bcd, d_pre_low)
    d_conv = (d_drive[...] * step + param_ref[6:7, :] * d_mixed) * conv_sig * (
        1.0 + conv * (1.0 - conv_sig)
    )
    x = inner_ref[...]
    shifted[0:chunk, :] = d_conv
    d_inner = param_ref[0:1, :] * d_conv
    d_param_ref[0:1, :] += jnp.sum(d_conv * x, axis=0, keepdims=True)
    for lag in range(1, 4):
        later = mask_ref[:, 3 + lag : 4 + lag] * shifted[lag : lag + chunk, :]
        d_inner += param_ref[lag : lag + 1, :] * later
        d_param_ref[lag : lag + 1, :] += jnp.sum(later * x, axis=0, keepdims=True)
    shifted[chunk : chunk + 8, :] = d_conv[0:8, :]
    d_inner_low = d_inner.astype(jnp.bfloat16)
    d_inner_ref[...] = d_inner_low
    d_param_ref[4:5, :] += jnp.sum(d_pre, axis=0, keepdims=True)
    d_param_ref[5:6, :] += jnp.sum(d_rate * step, axis=0, keepdims=True) * rate_scale
    d_param_ref[6:7, :] += jnp.sum(d_mixed * driven, axis=0, keepdims=True)
    carry_out[...] = carry[...]
    tail_out[...] = d_conv[0:8, :]
    part_ref[...] = (
        addend_ref[...].astype(jnp.float32)
        + dot_nt(d_inner_low, inner_w[...])
        + dot_nt(d_gate, gate_w[...])
        + dot_nt(d_bcd, bcd_w[...])
    ).astype(jnp.bfloat16)


def scan_backward(
    upstream, inner, gate, bcd, conv, mixed, addend, inner_w, gate_w, bcd_w, out_w, step_w, params, masks,
    starts, states, begin, end, earlier=None,
):
    length, width = upstream.shape
    channels = inner.shape[1]
    chunk = min(CHUNK, length)
    count = length // chunk
    features = bcd.shape[1]
    row = lambda i: (end - 1 - i, 0)
    fixed = lambda i: (0, 0)
    tall = pl.BlockSpec((chunk, channels), row)
    across = pl.BlockSpec((chunk, width), row)
    thin = pl.BlockSpec((chunk, features), row)
    pick_in, pick_out = picks(features, 0), picks(features, STATE)
    out_shape = [
        jax.ShapeDtypeStruct((length, channels), jnp.bfloat16),
        jax.ShapeDtypeStruct((length, channels), jnp.bfloat16),
        jax.ShapeDtypeStruct((length, features), jnp.bfloat16),
        jax.ShapeDtypeStruct((length, width), jnp.bfloat16),
        jax.ShapeDtypeStruct((features, channels), jnp.float32),
        jax.ShapeDtypeStruct((8, channels), jnp.float32),
        jax.ShapeDtypeStruct((STATE, channels), jnp.float32),
        jax.ShapeDtypeStruct((8, channels), jnp.float32),
    ]
    weights = [inner_w, gate_w, bcd_w, out_w, step_w, params]
    inputs = [upstream, inner, gate, bcd, conv, mixed, addend] + weights
    inputs += [masks, pick_in, pick_out, starts, states]
    if earlier is None:
        state_in = [
            jnp.zeros((STATE, channels), jnp.float32),
            jnp.zeros((8, channels), jnp.float32),
            jnp.zeros((features, channels), jnp.float32),
            jnp.zeros((8, channels), jnp.float32),
        ]
        filled = []
    else:
        state_in = [earlier[6], earlier[7], earlier[4], earlier[5]]
        filled = list(earlier[:4])
    inputs += state_in
    return pl.pallas_call(
        scan_backward_kernel,
        grid=(end - begin,),
        in_specs=[across, tall, tall, thin, tall, tall, across]
        + [whole(w) for w in weights]
        + [
            pl.BlockSpec((chunk, masks.shape[1]), row),
            whole(pick_in),
            whole(pick_out),
            pl.BlockSpec((1, STATE, channels), lambda i: (end - 1 - i, 0, 0)),
            pl.BlockSpec((chunk * STATE, channels), row),
        ]
        + [whole(v) for v in state_in]
        + [pl.BlockSpec(memory_space=pl.ANY)] * len(filled),
        out_specs=[
            tall,
            tall,
            thin,
            across,
            pl.BlockSpec((features, channels), fixed),
            pl.BlockSpec((8, channels), fixed),
            pl.BlockSpec((STATE, channels), fixed),
            pl.BlockSpec((8, channels), fixed),
        ],
        out_shape=out_shape,
        input_output_aliases={len(inputs) + i: i for i in range(len(filled))},
        scratch_shapes=[
            pltpu.VMEM((chunk + 8, channels), jnp.float32),
            pltpu.VMEM((chunk, channels), jnp.float32),
            pltpu.VMEM((chunk, channels), jnp.bfloat16),
            pltpu.VMEM((chunk, 256), jnp.bfloat16),
            pltpu.VMEM((chunk, 256), jnp.bfloat16),
            pltpu.VMEM((BLOCK * STATE, channels), jnp.float32),
            pltpu.VMEM((chunk, channels), jnp.bfloat16),
            pltpu.VMEM((BLOCK * STATE, channels), jnp.bfloat16),
            pltpu.VMEM((BLOCK * STATE, channels), jnp.bfloat16),
            pltpu.VMEM((chunk, channels), jnp.float32),
            pltpu.VMEM((chunk, channels), jnp.float32),
            pltpu.VMEM((STATE, channels), jnp.float32),
        ],
        compiler_params=pltpu.CompilerParams(vmem_limit_bytes=VMEM_LIMIT),
        cost_estimate=pl.CostEstimate(
            flops=length * channels * 120000 * (end - begin) // count,
            bytes_accessed=length * channels * 60,
            transcendentals=length * channels * 8,
        ),
        name="scan_backward",
    )(*inputs, *filled)


def scan_masks(segments):
    length = segments.shape[0]
    columns = []
    for lag in (1, 1, 2, 3):
        before = jnp.concatenate([jnp.full((lag,), -1, jnp.int32), segments[:-lag]])
        columns.append(before == segments)
    for lag in (1, 2, 3):
        after = jnp.concatenate([segments[lag:], jnp.full((lag,), -1, jnp.int32)])
        columns.append(after == segments)
    columns.append(jnp.zeros((length,), bool))
    return jnp.stack(columns, axis=1).astype(jnp.float32)


def attend_kernel(q_ref, kv_ref, bias_ref, out_ref, log_ref):
    heads = out_ref.shape[0] // HEAD_DIM
    groups = kv_ref.shape[0] // (2 * HEAD_DIM)
    repeat = heads // groups

    def group(g, _):
        span = pl.ds(pl.multiple_of(g * HEAD_DIM, HEAD_DIM), HEAD_DIM)
        second = pl.ds(pl.multiple_of((groups + g) * HEAD_DIM, HEAD_DIM), HEAD_DIM)
        keys = kv_ref[span, :].T
        vals = kv_ref[second, :]
        for r in range(repeat):
            head = g * repeat + r
            rows = pl.ds(pl.multiple_of(head * HEAD_DIM, HEAD_DIM), HEAD_DIM)
            scores = dot_nn(keys, q_ref[rows, :]) + bias_ref[...]
            peak = jnp.max(scores, axis=0, keepdims=True)
            probs = jnp.exp(scores - peak)
            total = jnp.sum(probs, axis=0, keepdims=True)
            mixed = dot_nn(vals, probs.astype(jnp.bfloat16)) / total
            out_ref[rows, :] = mixed.astype(out_ref.dtype)
            log_ref[pl.ds(head, 1), :] = peak + jnp.log(total)
        return 0

    lax.fori_loop(0, groups, group, 0)


def attend(q, kv, bias, heads):
    count = heads * q.shape[1] * kv.shape[1]
    return pl.pallas_call(
        attend_kernel,
        out_shape=[
            jax.ShapeDtypeStruct((heads * HEAD_DIM, q.shape[1]), jnp.bfloat16),
            jax.ShapeDtypeStruct((heads, q.shape[1]), jnp.float32),
        ],
        compiler_params=pltpu.CompilerParams(vmem_limit_bytes=VMEM_LIMIT),
        cost_estimate=pl.CostEstimate(flops=count * 2600, bytes_accessed=8 * q.size, transcendentals=count),
        name="attend",
    )(q, kv, bias)


def attend_back_kernel(
    q_ref, kv_ref, bias_ref, out_ref, log_ref, up_ref, dq_ref, dkv_ref
):
    heads = out_ref.shape[0] // HEAD_DIM
    groups = kv_ref.shape[0] // (2 * HEAD_DIM)
    repeat = heads // groups

    def group(g, _):
        span = pl.ds(pl.multiple_of(g * HEAD_DIM, HEAD_DIM), HEAD_DIM)
        second = pl.ds(pl.multiple_of((groups + g) * HEAD_DIM, HEAD_DIM), HEAD_DIM)
        keys_flat = kv_ref[span, :]
        keys = keys_flat.T
        vals = kv_ref[second, :].T
        d_keys = jnp.zeros(keys.shape, jnp.float32)
        d_vals = jnp.zeros(vals.shape, jnp.float32)
        for r in range(repeat):
            head = g * repeat + r
            rows = pl.ds(pl.multiple_of(head * HEAD_DIM, HEAD_DIM), HEAD_DIM)
            query = q_ref[rows, :]
            upstream = up_ref[rows, :]
            probs = jnp.exp(dot_nn(keys, query) + bias_ref[...] - log_ref[pl.ds(head, 1), :])
            level = jnp.sum(
                upstream.astype(jnp.float32) * out_ref[rows, :].astype(jnp.float32),
                axis=0,
                keepdims=True,
            )
            d_scores = (probs * (dot_nn(vals, upstream) - level)).astype(jnp.bfloat16)
            dq_ref[rows, :] = (dot_nn(keys_flat, d_scores) * HEAD_DIM**-0.5).astype(dq_ref.dtype)
            d_keys += dot_nt(d_scores, query)
            d_vals += dot_nt(probs.astype(jnp.bfloat16), upstream)
        dkv_ref[span, :] = d_keys.T.astype(dkv_ref.dtype)
        dkv_ref[second, :] = d_vals.T.astype(dkv_ref.dtype)
        return 0

    lax.fori_loop(0, groups, group, 0)


def attend_back(q, kv, bias, out, logs, upstream):
    heads = out.shape[0] // HEAD_DIM
    count = heads * q.shape[1] * kv.shape[1]
    return pl.pallas_call(
        attend_back_kernel,
        out_shape=[
            jax.ShapeDtypeStruct(out.shape, jnp.bfloat16),
            jax.ShapeDtypeStruct(kv.shape, jnp.bfloat16),
        ],
        compiler_params=pltpu.CompilerParams(vmem_limit_bytes=VMEM_LIMIT),
        cost_estimate=pl.CostEstimate(flops=count * 3000, bytes_accessed=16 * q.size, transcendentals=count),
        name="attend_back",
    )(q, kv, bias, out, logs, upstream)


def assemble_kernel(cuts, place_ref, *refs):
    pieces, outs, (held, in_sems, out_sems) = refs[:8], refs[8 : 8 + len(cuts)], refs[8 + len(cuts) :]
    ins = [
        [
            pltpu.make_async_copy(p.at[j], held.at[j, place_ref[k]], in_sems.at[j, k])
            for k, p in enumerate(pieces)
        ]
        for j in range(held.shape[0])
    ]
    stores = [
        pltpu.make_async_copy(held.at[j, :, :, begin:end], out, out_sems.at[i])
        for i, ((j, begin, end), out) in enumerate(zip(cuts, outs))
    ]
    for row in ins:
        for copy in row:
            copy.start()
    waited = 0
    for (j, _, _), store in zip(cuts, stores):
        while waited <= j:
            for copy in ins[waited]:
                copy.wait()
            waited += 1
        store.start()
    for store in stores:
        store.wait()


def assemble(pieces, places, cuts=None):
    count, rows, columns = pieces[0].shape
    if cuts is None:
        cuts = [(j, 0, columns) for j in range(count)]
    kind = pieces[0].dtype
    outs = pl.pallas_call(
        functools.partial(assemble_kernel, cuts),
        in_specs=[pl.BlockSpec(memory_space=pltpu.SMEM)] + [pl.BlockSpec(memory_space=pl.ANY)] * 8,
        out_specs=[pl.BlockSpec(memory_space=pl.ANY)] * len(cuts),
        out_shape=[jax.ShapeDtypeStruct((8, rows, end - begin), kind) for _, begin, end in cuts],
        scratch_shapes=[
            pltpu.VMEM((count, 8, rows, columns), kind),
            pltpu.SemaphoreType.DMA((count, 8)),
            pltpu.SemaphoreType.DMA((len(cuts),)),
        ],
        compiler_params=pltpu.CompilerParams(vmem_limit_bytes=VMEM_LIMIT),
        cost_estimate=pl.CostEstimate(flops=0, bytes_accessed=32 * pieces[0].size, transcendentals=0),
        name="assemble",
    )(places, *pieces)
    return [o.reshape(8 * rows, o.shape[2]) for o in outs]


def outer_kernel(count, flipped, place_ref, x_ref, *refs):
    d_refs, keep_ref, send_ref, total = refs[:count], refs[count], refs[count + 1], refs[count + 2]
    rows = total.shape[0] // 8
    for j in range(count):

        @pl.when(pl.program_id(0) == j)
        def _(j=j):
            total[...] = (dot_nn if flipped else dot_tn)(x_ref[...], d_refs[j][...])
            for k in range(8):
                block = total[pl.ds(pl.multiple_of(place_ref[k] * rows, rows), rows), :]
                out = keep_ref if k < 4 else send_ref
                out[0, (k % 4) * rows : (k % 4 + 1) * rows, :] = block.astype(jnp.bfloat16)


def outer(x, ds, places, flipped=False):
    width = x.shape[0] if flipped else x.shape[1]
    length, columns = ds[0].shape
    count = len(ds)
    spec = pl.BlockSpec((1, width // 2, columns), lambda j: (j, 0, 0))
    shape = jax.ShapeDtypeStruct((count, width // 2, columns), jnp.bfloat16)
    held = lambda array: pl.BlockSpec(array.shape, lambda j: (0, 0), pipeline_mode=pl.Buffered(1))
    return pl.pallas_call(
        functools.partial(outer_kernel, count, flipped),
        grid=(count,),
        in_specs=[pl.BlockSpec(memory_space=pltpu.SMEM), held(x)] + [held(d) for d in ds],
        out_specs=[spec, spec],
        out_shape=[shape, shape],
        scratch_shapes=[pltpu.VMEM((width, columns), jnp.float32)],
        compiler_params=pltpu.CompilerParams(vmem_limit_bytes=VMEM_LIMIT),
        cost_estimate=pl.CostEstimate(
            flops=4 * length * width * columns * count, bytes_accessed=4 * length * width, transcendentals=0
        ),
        name="outer",
    )(places, x, *ds)


def merge_kernel(parts, lows, *refs):
    total = refs[0][...].astype(jnp.float32)
    for ref in refs[1:parts]:
        total += ref[...].astype(jnp.float32)
    outs = refs[parts:]
    if lows:
        half = total.shape[1] // 2
        outs[0][...] = total[:, :half].astype(outs[0].dtype)
        outs[1][...] = total[:, half:].astype(outs[1].dtype)
    else:
        outs[0][...] = total.astype(outs[0].dtype)


def merge(parts, place, split):
    count, columns = parts[0].shape[0], parts[0].shape[2]
    rows = parts[1].shape[1] // 2
    specs = [
        pl.BlockSpec((1, rows, columns), (lambda j: (j, place, 0)) if p.shape[1] > rows else (lambda j: (j, 0, 0)))
        for p in parts
    ]
    out_rows = rows // 2 if split else rows
    out = pl.BlockSpec((1, out_rows, columns), lambda j: (j, 0, 0))
    shape = jax.ShapeDtypeStruct((count, out_rows, columns), jnp.bfloat16)
    return pl.pallas_call(
        functools.partial(merge_kernel, len(parts), split),
        grid=(count,),
        in_specs=specs,
        out_specs=[out] * (1 + split),
        out_shape=[shape] * (1 + split),
        compiler_params=pltpu.CompilerParams(vmem_limit_bytes=VMEM_LIMIT),
        cost_estimate=pl.CostEstimate(
            flops=0, bytes_accessed=8 * count * rows * columns, transcendentals=0
        ),
        name="merge",
    )(*parts)


def join_kernel(*refs):
    half = len(refs) // 2
    total = None
    for left_ref, right_ref in zip(refs[:half], refs[half : 2 * half]):
        part = dot_nt(left_ref[...], right_ref[...])
        total = part if total is None else total + part
    refs[-1][...] = total.astype(refs[-1].dtype)


def join(lefts, rights, tile=256):
    length = lefts[0].shape[0]
    width = rights[0].shape[0]
    tile = min(tile, length)
    row = lambda i: (i, 0)
    return pl.pallas_call(
        join_kernel,
        grid=(length // tile,),
        in_specs=[pl.BlockSpec((tile, l.shape[1]), row) for l in lefts] + [whole(r) for r in rights],
        out_specs=pl.BlockSpec((tile, width), row),
        out_shape=jax.ShapeDtypeStruct((length, width), jnp.bfloat16),
        compiler_params=pltpu.CompilerParams(vmem_limit_bytes=VMEM_LIMIT),
        cost_estimate=pl.CostEstimate(
            flops=4 * length * sum(r.size for r in rights),
            bytes_accessed=2 * length * width + sum(2 * r.size + 2 * l.size for l, r in zip(lefts, rights)),
            transcendentals=0,
        ),
        name="join",
    )(*lefts, *rights)


def feed_kernel(with_total, last, x_ref, d_act_ref, gate_w, up_w, *refs):
    act_ref, d_gate_ref, d_up_ref, d_x_ref = refs[-4:]
    x = x_ref[...]
    gate = dot_nn(x, gate_w[...])
    lift = dot_nn(x, up_w[...])
    d_act = d_act_ref[...].astype(jnp.float32)
    sig = sigmoid(gate)
    silu = gate * sig
    act_ref[...] = (silu * lift).astype(jnp.bfloat16)
    d_gate = (d_act * lift * sig * (1.0 + gate * (1.0 - sig))).astype(jnp.bfloat16)
    d_up = (d_act * silu).astype(jnp.bfloat16)
    d_gate_ref[...] = d_gate
    d_up_ref[...] = d_up
    d_x = dot_nt(d_gate, gate_w[...]) + dot_nt(d_up, up_w[...])
    if with_total:
        d_x = d_x + refs[0][...]
    d_x_ref[...] = d_x.astype(d_x_ref.dtype)


def feed(x, d_act, gate_w, up_w, begin, total=None, last=True, earlier=()):
    length, width = x.shape
    rows, units = d_act.shape
    tile = min(256, length)
    first = begin // tile
    here = pl.BlockSpec((tile, width), lambda i: (i, 0))
    tall = pl.BlockSpec((tile, units), lambda i: (first + i, 0))
    filled = list(earlier)
    inputs = [x, d_act, gate_w, up_w] + ([] if total is None else [total])
    return pl.pallas_call(
        functools.partial(feed_kernel, total is not None, last),
        grid=(length // tile,),
        in_specs=[here, tall, whole(gate_w), whole(up_w)]
        + [here] * (total is not None)
        + [pl.BlockSpec(memory_space=pl.ANY)] * len(filled),
        out_specs=[tall] * 3 + [here],
        out_shape=[jax.ShapeDtypeStruct((rows, units), jnp.bfloat16)] * 3
        + [jax.ShapeDtypeStruct((length, width), jnp.bfloat16 if last else jnp.float32)],
        input_output_aliases={len(inputs) + i: i for i in range(len(filled))},
        compiler_params=pltpu.CompilerParams(vmem_limit_bytes=VMEM_LIMIT),
        cost_estimate=pl.CostEstimate(
            flops=13 * length * gate_w.size,
            bytes_accessed=4 * gate_w.size + 6 * length * (width + units),
            transcendentals=length * units,
        ),
        name="feed",
    )(*inputs, *filled)


def inverse_rms(values):
    return lax.rsqrt(jnp.mean(values * values, axis=-1, keepdims=True) + epsilon)


def norm_backward(values, inv_scale, gain_vec, upstream):
    weighted = upstream * gain_vec
    d_values = inv_scale * weighted - values * inv_scale**3 * jnp.mean(
        values * weighted, axis=-1, keepdims=True
    )
    return (d_values, jnp.sum(upstream * values * inv_scale, axis=0))


def contract(pattern, left_side, right_side):
    return jnp.einsum(pattern, left_side, right_side, preferred_element_type=jnp.float32)


def low(values):
    return values.astype(jnp.bfloat16)


def hop_first(shard):
    return lax.ppermute(shard, "dp", [(i, i ^ (2 if i & 1 else 4)) for i in range(8)])


def hop_second(shard):
    return lax.ppermute(shard, "dp", [(i, i ^ (4 if i & 1 else 2)) for i in range(8)])


def hop_core(shard):
    return lax.ppermute(shard, "dp", [(i, i ^ 1) for i in range(8)])


class Gather:
    def __init__(self, shard):
        self.shard = shard
        self.direct = lax.axis_size("dp") != 8

    def begin(self):
        if not self.direct:
            self.first = hop_first(self.shard)
            self.second = hop_second(self.shard)

    def cross(self):
        if not self.direct:
            self.third = hop_second(self.first)
            self.core_own = hop_core(self.shard)
            self.core_first = hop_core(self.first)
            self.core_second = hop_core(self.second)

    def finish(self):
        if not self.direct:
            self.core_third = hop_core(self.third)

    def rows(self, places, cuts=None):
        if self.direct:
            arrays = list(lax.all_gather(self.shard, "dp", axis=1, tiled=True))
            return arrays if cuts is None else [arrays[j][:, begin:end] for j, begin, end in cuts]
        own = [self.shard, self.first, self.second, self.third]
        return assemble(
            own + [self.core_own, self.core_first, self.core_second, self.core_third], places, cuts
        )


STEP_1 = "first second"
STEP_2 = "third core_own core_first core_second"
STEP_3 = "core_third"


def sum_tensor(values):
    ways = lax.axis_size("tensor")
    step = 1
    while step < ways:
        pairs = [(i, i ^ step) for i in range(ways)]
        values = values + lax.ppermute(low(values), "tensor", pairs).astype(jnp.float32)
        step *= 2
    return values


class RowSum:
    def __init__(self, keep, send):
        self.whole = lax.axis_size("dp") == 8
        self.keep = keep
        self.send = send

    def begin(self):
        if self.whole:
            self.other = hop_core(self.send)

    def second(self):
        if not self.whole:
            return
        (high,) = merge([self.keep, self.other], 1, False)
        self.across = hop_second(high)

    def third(self):
        if not self.whole:
            return
        self.base, high = merge([self.keep, self.other, self.across], 0, True)
        self.near = hop_first(high)

    def result(self):
        if not self.whole:
            rows = jnp.concatenate([self.keep, self.send], -2)
            return lax.psum_scatter(
                rows, "dp", scatter_dimension=rows.ndim - 2, tiled=True
            ).astype(jnp.float32)
        return self.base.astype(jnp.float32) + self.near.astype(jnp.float32)


def sync(moves, *values):
    places = [
        (item, name)
        for items, names in moves
        for item in items
        for name in names.split()
        if hasattr(item, name)
    ]
    arrays, values = lax.optimization_barrier(([getattr(i, n) for i, n in places], values))
    for (item, name), array in zip(places, arrays):
        setattr(item, name, array)
    return values[0] if len(values) == 1 else values


def block_places():
    if lax.axis_size("dp") != 8:
        return jnp.arange(8, dtype=jnp.int32)
    rank = lax.axis_index("dp").astype(jnp.int32)
    even, odd = jnp.array(EVEN_ORDER, jnp.int32), jnp.array(ODD_ORDER, jnp.int32)
    return rank ^ jnp.where(rank & 1 == 1, odd, even)


def shards(
    hidden_in,
    out_grad,
    segments,
    norm_input,
    query_weight,
    key_weight,
    value_weight,
    attn_out_weight,
    norm_attn,
    ssm_x_weight,
    ssm_gate_weight,
    ssm_bcd_weight,
    step_weight,
    step_bias,
    decay_log,
    skip_gain,
    conv_weight,
    ssm_out_weight,
    norm_ssm,
    norm_ffn,
    gate_weight,
    up_weight,
    down_weight,
):
    tokens, width = hidden_in.shape
    data_ways = lax.axis_size("dp")
    tensor_ways = lax.axis_size("tensor")
    tensor_rank = lax.axis_index("tensor")
    channels = ssm_x_weight.shape[1]
    rank_rows = step_weight.shape[0]
    taps = conv_weight.shape[0]
    owned = step_weight.shape[1]
    spans = channels // owned
    group = segments.shape[0]

    places = block_places()
    paired = tensor_ways == 4

    def swap(values, step):
        return lax.ppermute(values, "tensor", [(i, i ^ step) for i in range(tensor_ways)])

    small = jnp.concatenate(
        [step_weight, step_bias[None], decay_log[None], skip_gain[None], conv_weight], axis=0
    )
    small_rows = small.shape[0]
    block_rows = width // data_ways
    gain_columns = jnp.stack([norm_input, norm_attn, norm_ssm, norm_ffn], axis=1)
    bcd_columns = ssm_bcd_weight.shape[1]
    features = bcd_columns + 4
    thin = jnp.concatenate([ssm_bcd_weight, gain_columns, small.reshape(block_rows, -1)], axis=1)
    key_width = key_weight.shape[1]
    query_width = query_weight.shape[1]
    query_end = 2 * key_width + -(-query_width // 128) * 128
    mid = jnp.concatenate(
        [
            key_weight,
            value_weight,
            jnp.pad(query_weight, ((0, 0), (0, query_end - 2 * key_width - query_width))),
            attn_out_weight,
        ],
        axis=1,
    )
    mid_cuts = [
        (0, 0, 2 * key_width),
        (0, 2 * key_width, query_end),
        (0, query_end, mid.shape[1]),
    ]

    all_hidden = lax.all_gather(hidden_in, "tensor", axis=0, tiled=True)
    scan_move = Gather(jnp.stack([ssm_x_weight, ssm_gate_weight, ssm_out_weight.T]))
    scan_move.begin()
    thin_move = Gather(thin[None])
    mid_move = Gather(mid[None])
    ffn_move = Gather(jnp.stack([gate_weight, up_weight, down_weight.T]))
    masks = scan_masks(segments)
    query_pos = tensor_rank * tokens + jnp.arange(tokens, dtype=jnp.int32)
    key_pos = jnp.arange(group, dtype=jnp.int32)
    query_seg = lax.dynamic_slice_in_dim(segments, tensor_rank * tokens, tokens, 0)
    allowed = (
        (key_pos[:, None] <= query_pos[None, :])
        & (query_pos[None, :] - key_pos[:, None] < WINDOW)
        & (segments[:, None] == query_seg[None, :])
    )
    bias = jnp.where(allowed, 0.0, -1e30)

    far_pieces = [None] * 3
    masks, bias = sync(
        [([scan_move], STEP_1), ([thin_move, mid_move, ffn_move], "shard")], masks, bias
    )
    scan_move.cross()
    thin_move.begin()
    masks = sync([([scan_move], STEP_2), ([thin_move], STEP_1)], masks)
    scan_move.finish()
    thin_move.cross()
    masks = sync([([scan_move], STEP_3), ([thin_move], STEP_2)], masks)
    thin_move.finish()
    mid_move.begin()
    if paired:
        far_pieces[0] = swap(ffn_move.shard[:1], 2)
    x_all, ssm_gate_all, ssm_out_all = scan_move.rows(places)
    x_all, ssm_gate_all, ssm_out_all = sync(
        [([thin_move], STEP_3)], x_all, ssm_gate_all, ssm_out_all
    )
    (thin_all,) = thin_move.rows(places)
    gains_f32 = thin_all[:, bcd_columns:features].T.astype(jnp.float32)
    gain_input, gain_attn, gain_ssm, gain_ffn = (gains_f32[i] for i in range(4))
    bcd_all = thin_all[:, :features]
    small_local = lax.dynamic_slice_in_dim(
        thin_all.reshape(data_ways, block_rows, -1), tensor_rank * spans, spans, 0
    )[:, :, features:]
    small_local = small_local.reshape(spans, small_rows, owned)
    small_local = small_local.transpose(1, 0, 2).reshape(small_rows, channels)
    small_f32 = small_local[rank_rows:].astype(jnp.float32)
    params = jnp.concatenate(
        [
            small_f32[3:],
            small_f32[0:1],
            jnp.exp(small_f32[1:2]),
            small_f32[2:3],
            jnp.zeros((1, channels), jnp.float32),
        ]
    )
    step_pad = jnp.pad(small_local[:rank_rows], ((2 * STATE, 4), (0, 0)))
    (
        all_hidden, gain_row, x_all, ssm_gate_all, bcd_all, ssm_out_all, step_pad, params, masks, far_pieces,
    ) = sync(
        [([ffn_move], "shard")],
        all_hidden,
        gain_input[None],
        x_all,
        ssm_gate_all,
        bcd_all,
        ssm_out_all,
        step_pad,
        params,
        masks,
        far_pieces,
    )

    ffn_move.begin()
    if paired:
        far_pieces[1] = swap(ffn_move.shard[1:2], 2)
    forward_inputs = (
        all_hidden, gain_row, x_all, ssm_gate_all, bcd_all, ssm_out_all, step_pad, params, masks,
    )
    chunks = max(group // CHUNK, 1)
    half = chunks // 2
    former = scan_forward(*forward_inputs, 0, half)
    former, far_pieces = sync([([mid_move], STEP_1)], tuple(former), far_pieces)
    mid_move.cross()
    if paired:
        far_pieces[2] = swap(ffn_move.shard[2:], 2)
    (
        all_normed, inner_in, gate_in, bcd_low, conv_total, mixed_total, gated_low, starts, states, ssm_part,
    ) = scan_forward(*forward_inputs, half, chunks, former)[:10]
    ssm_part, all_normed, far_pieces = sync(
        [([mid_move], STEP_2), ([ffn_move], STEP_1)], ssm_part, all_normed, far_pieces
    )
    ssm_proj = lax.psum_scatter(ssm_part, "tensor", scatter_dimension=0, tiled=True)
    mid_move.finish()
    far_moves = []
    if paired:
        far_move = Gather(jnp.concatenate(far_pieces))
        far_moves = [far_move]
    all_normed = sync([([mid_move], STEP_3), (far_moves, "shard")], all_normed)
    ffn_move.cross()

    normed = lax.dynamic_slice_in_dim(all_normed, tensor_rank * tokens, tokens, 0)
    kv_all, query_all, attn_out_all = mid_move.rows(places, mid_cuts)
    kv = low(contract("td,de->et", all_normed, kv_all))
    queries = low(low(contract("td,de->et", normed, query_all)) * HEAD_DIM**-0.5)
    queries, kv = sync([([ffn_move], STEP_2)], queries, kv)
    ffn_move.finish()
    if paired:
        out_grad_near = swap(out_grad, 1)
        far_move.begin()
    attended, log_totals = attend(queries, kv, bias, query_width // HEAD_DIM)
    if paired:
        attended, out_grad_near = sync([([ffn_move], STEP_3)], attended, out_grad_near)
        ffn_out_grad = jnp.concatenate([out_grad, out_grad_near])
    else:
        ffn_out_grad = lax.all_gather(out_grad, "tensor", axis=0, tiled=True)
    attn_proj = contract("et,ed->td", attended, attn_out_all)
    scale_attn = inverse_rms(attn_proj)
    residual_half = hidden_in.astype(jnp.float32) + 0.5 * attn_proj * scale_attn * gain_attn
    gate_all, up_all, down_all = ffn_move.rows(places)
    d_act = low(contract("gd,df->gf", ffn_out_grad, down_all))

    ssm_proj, residual_half, d_act, gate_all, up_all = sync(
        [(far_moves, STEP_1)], ssm_proj, residual_half, d_act, gate_all, up_all
    )
    for g in far_moves:
        g.cross()
    ssm_proj = ssm_proj.astype(jnp.float32)
    scale_ssm = inverse_rms(ssm_proj)
    residual = residual_half + 0.5 * ssm_proj * scale_ssm * gain_ssm
    scale_ffn = inverse_rms(residual)
    ffn_in = low(residual * scale_ffn * gain_ffn)
    if paired:
        ffn_near = swap(ffn_in, 1)
        own = feed(ffn_in, d_act, gate_all, up_all, 0, last=False)
        ffn_near, own = sync([(far_moves, STEP_2)], ffn_near, tuple(own))
        far_move.finish()
        near = feed(ffn_near, d_act, gate_all, up_all, tokens, last=False, earlier=own[:-1])
        near, own_total = sync([(far_moves, STEP_3)], tuple(near), own[-1])
        gate_far, up_far, down_far = far_move.rows(places)
        d_act_far = low(contract("gd,df->gf", ffn_out_grad, down_far))
        far = feed(ffn_near, d_act_far, gate_far, up_far, tokens, near[-1])
        far, own_total = sync([], tuple(far), own_total)
        arrived = swap(far[-1], 1)
        both = feed(ffn_in, d_act_far, gate_far, up_far, 0, own_total, earlier=far[:-1])
        ffn_rows = jnp.concatenate([ffn_in, ffn_near])
        both = sync([], tuple(both))
        activated, d_gates, d_ups = ([near[i], both[i]] for i in range(3))
        own_part = both[-1]
        down_parts = (down_all, down_far)
    else:
        ffn_rows = lax.all_gather(ffn_in, "tensor", axis=0, tiled=True)
        near = feed(ffn_rows, d_act, gate_all, up_all, 0)
        activated, d_gates, d_ups = ([near[i]] for i in range(3))
        own_part = near[-1]
        down_parts = (down_all,)

    sum_down = RowSum(*outer(ffn_out_grad, activated, places))
    if paired:
        arrived = sync([([sum_down], "keep send")], arrived)
        d_ffn_in = own_part.astype(jnp.float32) + arrived.astype(jnp.float32)
    else:
        d_ffn_in = lax.psum_scatter(own_part, "tensor", scatter_dimension=0, tiled=True)
        d_ffn_in = d_ffn_in.astype(jnp.float32)
    sum_down.begin()

    d_res_norm, grad_gain_ffn = norm_backward(residual, scale_ffn, gain_ffn, d_ffn_in)
    d_residual = out_grad.astype(jnp.float32) + d_res_norm
    d_attn_proj, grad_gain_attn = norm_backward(attn_proj, scale_attn, gain_attn, 0.5 * d_residual)
    d_ssm_proj, grad_gain_ssm = norm_backward(ssm_proj, scale_ssm, gain_ssm, 0.5 * d_residual)
    d_ssm_low = low(d_ssm_proj)
    all_ssm_grad = lax.all_gather(d_ssm_low, "tensor", axis=0, tiled=True)

    d_attn_low, _ = sync([], low(d_attn_proj), d_ssm_low)
    d_attended = low(contract("td,cd->ct", d_attn_low, attn_out_all))
    sum_attn_out = RowSum(*outer(attended, [d_attn_low], places, flipped=True))
    d_attended = sync([([sum_down], "other"), ([sum_attn_out], "keep send")], d_attended)
    sum_attn_out.begin()
    sum_down.second()
    d_queries, d_kv = attend_back(queries, kv, bias, attended, log_totals, d_attended)
    d_queries, d_kv = sync([([sum_attn_out], "other")], d_queries.T, d_kv.T)
    sum_attn_out.second()
    sums_attn = [
        RowSum(*outer(normed, [d_queries], places)),
        RowSum(*outer(all_normed, [d_kv], places)),
    ]
    d_gates, d_ups, d_kv = sync(
        [(sums_attn, "keep send"), ([sum_down], "across")], tuple(d_gates), tuple(d_ups), d_kv
    )
    for s in sums_attn:
        s.begin()
    sum_down.third()
    sum_gate = RowSum(*outer(ffn_rows, d_gates, places))
    d_ups, d_kv = sync(
        [(sums_attn, "other"), ([sum_gate], "keep send"), ([sum_attn_out], "across")], d_ups, d_kv
    )
    for s in sums_attn:
        s.second()
    sum_gate.begin()
    sum_attn_out.third()
    sum_up = RowSum(*outer(ffn_rows, d_ups, places))
    kv_part = low(contract("te,de->td", d_kv, kv_all))
    all_ssm_grad, kv_part = sync(
        [
            ([sum_gate], "other"),
            ([sum_up], "keep send"),
            ([sum_down, sum_attn_out], "near"),
            (sums_attn, "across"),
        ],
        all_ssm_grad,
        kv_part,
    )

    for s in sums_attn:
        s.third()
    sum_up.begin()
    sum_gate.second()
    grad_down = sum_down.result()
    if paired:
        grad_down_far = swap(low(grad_down[1]), 2)
    scan_inputs = (
        all_ssm_grad, inner_in, gate_in, bcd_low, conv_total, mixed_total, kv_part,
        x_all, ssm_gate_all, bcd_all, ssm_out_all, step_pad, params, masks, starts, states,
    )
    later = scan_backward(*scan_inputs, half, chunks)
    later = sync(
        [(sums_attn, "near"), ([sum_gate], "across"), ([sum_up], "other")], tuple(later)
    )
    attn_grads = lax.psum([low(s.result()[0]) for s in sums_attn + [sum_attn_out]], "tensor")
    sum_gate.third()
    sum_up.second()
    d_inner, d_gate_in, d_bcd, d_normed_part, d_step_pad, d_params = scan_backward(
        *scan_inputs, 0, half, later
    )[:6]
    d_normed_part, d_inner, d_gate_in, d_bcd, attn_grads = sync(
        [([sum_gate], "near"), ([sum_up], "across")],
        d_normed_part,
        d_inner,
        d_gate_in,
        d_bcd,
        tuple(attn_grads),
    )
    d_normed_sum = lax.psum_scatter(d_normed_part, "tensor", scatter_dimension=0, tiled=True)

    sum_up.third()
    grad_gate = sum_gate.result()
    if paired:
        grad_gate_far = swap(low(grad_gate[1]), 2)
    sum_in = RowSum(*outer(all_normed, [d_inner, d_gate_in], places))
    d_bcd, gated_late = sync([([sum_in], "keep send"), ([sum_up], "near")], d_bcd, gated_low)
    sum_in.begin()
    grad_up = sum_up.result()
    if paired:
        grad_up_far = swap(low(grad_up[1]), 2)
    sum_out = RowSum(*outer(all_ssm_grad, [gated_late], places))
    grad_bcd = contract("gd,gc->dc", all_normed, d_bcd)
    d_normed_own = contract("te,de->td", d_queries, query_all[:, :query_width])
    grad_gain_input = (
        jnp.sum(d_normed_part.astype(jnp.float32) * all_normed.astype(jnp.float32), axis=0)
        + jnp.sum(d_normed_own * normed.astype(jnp.float32), axis=0)
    ) / gain_input
    d_gains = jnp.stack([grad_gain_input, grad_gain_attn, grad_gain_ssm, grad_gain_ffn], axis=1)
    d_small = jnp.concatenate(
        [d_step_pad[2 * STATE : 2 * STATE + rank_rows], d_params[4:7], d_params[:taps]], axis=0
    )
    d_small = low(d_small.reshape(small_rows, spans, owned).transpose(1, 0, 2))
    d_small = lax.dynamic_update_slice_in_dim(
        jnp.zeros((data_ways, block_rows, small_rows * owned // block_rows), jnp.bfloat16),
        d_small.reshape(spans, block_rows, -1),
        tensor_rank * spans,
        0,
    )
    d_thin = jnp.concatenate(
        [low(grad_bcd[:, :bcd_columns]), low(d_gains), d_small.reshape(width, -1)], axis=1
    )
    if data_ways == 8:
        d_thin = d_thin.reshape(data_ways, block_rows, -1)
        d_thin = jnp.concatenate([lax.dynamic_index_in_dim(d_thin, places[k], 0, False) for k in range(8)])
    sum_thin = RowSum(d_thin[None, : width // 2], d_thin[None, width // 2 :])
    activated = sync([([sum_out, sum_thin], "keep send"), ([sum_in], "other")], tuple(activated))
    sum_in.second()
    sum_out.begin()
    sum_thin.begin()
    ffn_part = join(activated, down_parts)
    ffn_part = sync([([sum_out, sum_thin], "other"), ([sum_in], "across")], ffn_part)
    if paired:
        ffn_out_near = swap(ffn_part[tokens:], 1)
    sum_in.third()
    sum_out.second()
    sum_thin.second()
    ffn_part = sync([([sum_out, sum_thin], "across")], ffn_part)
    sum_out.third()
    sum_thin.third()
    if paired:
        ffn_out = ffn_part[:tokens].astype(jnp.float32) + ffn_out_near.astype(jnp.float32)
    else:
        ffn_out = lax.psum_scatter(ffn_part, "tensor", scatter_dimension=0, tiled=True)
    layer_out = low(residual + ffn_out.astype(jnp.float32))
    (grad_x, grad_ssm_gate), (grad_ssm_out,), (d_thin,) = (
        s.result() for s in (sum_in, sum_out, sum_thin)
    )
    d_thin = sum_tensor(d_thin)
    if paired:
        grad_down_far, grad_gate_far, grad_up_far, layer_out, d_thin = sync(
            [], grad_down_far, grad_gate_far, grad_up_far, layer_out, d_thin
        )
        grad_down = grad_down[0] + grad_down_far.astype(jnp.float32)
        grad_gate = grad_gate[0] + grad_gate_far.astype(jnp.float32)
        grad_up = grad_up[0] + grad_up_far.astype(jnp.float32)
    else:
        grad_down, grad_gate, grad_up = grad_down[0], grad_gate[0], grad_up[0]
    grad_bcd = d_thin[:, :bcd_columns]
    d_gains = d_thin[:, bcd_columns:features].T
    d_small_own = d_thin[:, features:].reshape(small_rows, owned)

    hidden_f32 = hidden_in.astype(jnp.float32)
    scale_in = inverse_rms(hidden_f32)
    d_normed = d_normed_sum.astype(jnp.float32) + d_normed_own
    d_input_norm, _ = norm_backward(hidden_f32, scale_in, gain_input, d_normed)
    grad_input = d_residual + d_input_norm
    grad_query, grad_kv, grad_attn_out = (v.astype(jnp.float32) for v in attn_grads)
    return (
        layer_out,
        grad_input,
        d_gains[0],
        grad_query,
        grad_kv[:, :key_width],
        grad_kv[:, key_width:],
        grad_attn_out,
        d_gains[1],
        grad_x,
        grad_ssm_gate,
        grad_bcd,
        d_small_own[:rank_rows],
        d_small_own[rank_rows],
        d_small_own[rank_rows + 1],
        d_small_own[rank_rows + 2],
        d_small_own[rank_rows + 3 :],
        grad_ssm_out.T,
        d_gains[2],
        d_gains[3],
        grad_gate,
        grad_up,
        grad_down.T,
    )


def solution(mesh):
    rows = P(("dp", "tensor"), None)
    both = P("dp", "tensor")
    in_specs = (
        rows,
        rows,
        P("dp"),
        P("dp"),
        P("dp", None),
        P("dp", None),
        P("dp", None),
        P("dp", None),
        P("dp"),
        both,
        both,
        P("dp", None),
        P(None, "dp"),
        P("dp"),
        P("dp"),
        P("dp"),
        P(None, "dp"),
        P("tensor", "dp"),
        P("dp"),
        P("dp"),
        both,
        both,
        P("tensor", "dp"),
    )
    out_specs = (
        rows,
        rows,
        P("dp"),
        P("dp", None),
        P("dp", None),
        P("dp", None),
        P("dp", None),
        P("dp"),
        both,
        both,
        P("dp", None),
        P(None, "dp"),
        P("dp"),
        P("dp"),
        P("dp"),
        P(None, "dp"),
        P("tensor", "dp"),
        P("dp"),
        P("dp"),
        both,
        both,
        P("tensor", "dp"),
    )
    return jax.shard_map(shards, mesh=mesh, in_specs=in_specs, out_specs=out_specs, check_vma=False)
```
